256 devices in a mesh: dp: 2 (over core), ctx: 8 (over z), tp: 16 (over y, x).
Axes of the slice: x: 4, y: 4, z: 8, core: 2. Of those that a mesh axis runs over, the one named last changes fastest.
Arguments:
- queries: bfloat16 [16384, 4096], P(('dp', 'ctx'), 'tp'), parts along dimension 0, may hold values from -1.5 to 1.5
- keys: bfloat16 [16384, 4096], P(('dp', 'ctx'), 'tp'), parts along dimension 0, may hold values from -1.5 to 1.5
- values: bfloat16 [16384, 8192], P(('dp', 'ctx'), 'tp'), parts along dimension 0, may hold values from -25 to 25
- gates: bfloat16 [16384, 8192], P(('dp', 'ctx'), 'tp'), parts along dimension 0, may hold values from -6 to 6
- decay_log: float32 [16, 16384], P('tp', ('dp', 'ctx')), parts along dimension 1, may hold values from -2.5 to 0
- out_weight: bfloat16 [8192, 4096], P('tp'), may hold values from -0.09375 to 0.09375
Outputs:
- mixed: bfloat16 [16384, 4096], P(('dp', 'ctx'), 'tp'), parts along dimension 0
The draws below stay inside these ranges and needn't reach their ends.
There are 2 independent parts, one for each index of `dp`. The reference program is written for one: setup_inputs(seed, part) draws one part's arguments, and reference() takes and returns one part's arrays. A program takes and returns all parts, laid end to end along the dimension named above; an argument that names none is the same for every part. Nothing has to cross between parts.
All inputs are finite; a program needn't handle non-finite values.
Results may differ from the reference program's by a relative error of at most 0.0058.
Values may be sent and summed in bfloat16 or wider, within the bound.
A program may use at most 128 MiB of HBM per device.

```python
import math
import jax
import jax.numpy as jnp
from jax import lax

D = 4096
RETENTION_HEADS = 16
DK = 256
DV = 512
TOK_DEV = 1024
WINDOW_LENGTH = 8192


def draw_values(key, part):
    key = jax.random.fold_in(key, 11)
    first, second, third = jax.random.split(key, 3)
    column_scale = jnp.exp(jax.random.uniform(second, (1, RETENTION_HEADS * DV), jnp.float32, 0.0, math.log(10.0)))
    row_scale = jnp.exp(jax.random.uniform(third, (WINDOW_LENGTH, 1), jnp.float32, 0.0, math.log(10.0)))
    base = jax.random.truncated_normal(first, -2.2, 2.2, (WINDOW_LENGTH, RETENTION_HEADS * DV), jnp.float32)
    return (base * column_scale * row_scale * 0.1).astype(jnp.bfloat16)


def draw_decay_log(key, part):
    key = jax.random.fold_in(key, 23)
    split_key_parts = jax.random.split(key, 7)
    blocks = WINDOW_LENGTH // TOK_DEV
    quick_head = jax.random.randint(split_key_parts[0], (RETENTION_HEADS, 1), 0, 2) == 1
    slow_rate = jnp.exp(jax.random.uniform(split_key_parts[1], (RETENTION_HEADS, 1), jnp.float32, math.log(0.05), math.log(0.3))) / WINDOW_LENGTH
    quick_rate = jnp.exp(jax.random.uniform(split_key_parts[2], (RETENTION_HEADS, 1), jnp.float32, math.log(0.03), math.log(0.08)))
    head_decay_rate = jnp.where(quick_head, quick_rate, slow_rate)
    shard_decay_factor = jnp.exp(jax.random.uniform(split_key_parts[3], (RETENTION_HEADS, blocks), jnp.float32, math.log(0.5), math.log(2.0)))
    shard_decay_factor = jnp.repeat(shard_decay_factor, TOK_DEV, axis=1)
    per_token_factor = jax.random.uniform(split_key_parts[4], (RETENTION_HEADS, WINDOW_LENGTH), jnp.float32, 0.5, 1.5)
    spike_position = jax.random.randint(split_key_parts[5], (RETENTION_HEADS, 3), 0, WINDOW_LENGTH)
    spike_retained_factor = jax.random.uniform(split_key_parts[6], (RETENTION_HEADS, 3), jnp.float32, 0.6, 0.8)
    token_positions = jnp.arange(WINDOW_LENGTH, dtype=jnp.int32)
    match_count = token_positions[None, :, None] == spike_position[:, None, :]
    spike_decay = jnp.sum(jnp.where(match_count, jnp.log(spike_retained_factor)[:, None, :], 0.0), axis=-1)
    return (-head_decay_rate * shard_decay_factor * per_token_factor + spike_decay).astype(jnp.float32)


def with_spikes(result, rng, source, target, parts, factor):
    owner, partner = [(jnp.arange(result.shape[axis_at]) // (result.shape[axis_at] // parts)).reshape([-1 if axis == axis_at else 1 for axis in range(result.ndim)]) for axis_at in (source, target)]
    chosen = jax.random.permutation(rng, parts)[partner]
    strong = (owner == chosen) | (owner == (partner + parts // 2) % parts)
    return jnp.where(strong, factor * result, result)


def shard_levels(own_key, dims, cuts, least, high):
    factor_of = 1.0
    for dim, parts in cuts:
        draws = jax.random.uniform(jax.random.fold_in(jax.random.fold_in(own_key, 6), dim), (parts,), jnp.float32, least / len(cuts), high / len(cuts))
        factor_of = factor_of * jnp.repeat(jnp.exp(draws), dims[dim] // parts).reshape((-1,) + (1,) * (len(dims) - 1 - dim))
    return factor_of


def centred(key, extent, scale, reach, pieces=(), held_as=jnp.bfloat16):
    drawn = scale * jax.random.normal(key, extent, jnp.float32)
    if pieces:
        drawn = drawn * shard_levels(key, extent, pieces, -0.22, 0.18)
    return jnp.clip(drawn, -reach, reach).astype(held_as)


def gaussian_with(own_key, shape, scale, bound, shards, heavy, kind=jnp.bfloat16):
    entries = scale * jax.random.normal(own_key, shape, jnp.float32)
    if shards:
        entries = entries * shard_levels(own_key, shape, shards, -0.22, 0.18)
    return jnp.clip(with_spikes(entries, jax.random.fold_in(own_key, 3), *heavy), -bound, bound).astype(kind)


def setup_inputs(seed: int = 0, part: int = 0) -> dict:
    seeds = jax.random.split(jax.random.key(seed), 7)
    own_keys = jax.random.split(jax.random.fold_in(seeds[6], part), 7)
    return {
        "queries": centred(own_keys[0], (WINDOW_LENGTH, RETENTION_HEADS * DK), 0.25, 1.5, ((0, 8), (1, 16))),
        "keys": centred(own_keys[1], (WINDOW_LENGTH, RETENTION_HEADS * DK), 0.25, 1.5, ((0, 8), (1, 16))),
        "values": draw_values(jax.random.fold_in(jax.random.fold_in(seeds[6], part), 71), part),
        "gates": centred(own_keys[3], (WINDOW_LENGTH, RETENTION_HEADS * DV), 1.0, 6.0, ((0, 8), (1, 16))),
        "decay_log": draw_decay_log(jax.random.fold_in(jax.random.fold_in(seeds[6], part), 71), part),
        "out_weight": gaussian_with(seeds[5], (RETENTION_HEADS * DV, D), (RETENTION_HEADS * DV) ** -0.5, 0.09375, ((0, 16),), (0, 1, 16, 2.0)),
    }


def block_pieces(query_block, key_block, value_block, decay_block):
    count = query_block.shape[0]
    cumulative = jnp.cumsum(decay_block)
    causal = lax.broadcasted_iota(jnp.int32, (count, count), 0) >= lax.broadcasted_iota(jnp.int32, (count, count), 1)
    spread = cumulative[:, None] - cumulative[None, :]
    decay_weight = jnp.exp(jnp.where(causal, spread, -1e+30))
    scores = jnp.dot(query_block, key_block.T, preferred_element_type=jnp.float32)
    masked = (scores * decay_weight).astype(jnp.bfloat16)
    intra = jnp.dot(masked, value_block, preferred_element_type=jnp.float32)
    block_total = cumulative[-1]
    decay_weighted_keys = (key_block.astype(jnp.float32) * jnp.exp(block_total - cumulative)[:, None]).astype(jnp.bfloat16)
    block_state = jnp.dot(decay_weighted_keys.T, value_block, preferred_element_type=jnp.float32)
    query_decayed = query_block.astype(jnp.float32) * jnp.exp(cumulative)[:, None]
    return (intra, query_decayed, block_state, block_total)

def reference(queries, keys, values, gates, decay_log, out_weight):
    length = queries.shape[0]
    blocks = length // TOK_DEV
    query_all = queries.reshape(blocks, TOK_DEV, RETENTION_HEADS, DK).transpose(2, 0, 1, 3)
    key_all = keys.reshape(blocks, TOK_DEV, RETENTION_HEADS, DK).transpose(2, 0, 1, 3)
    value_all = values.reshape(blocks, TOK_DEV, RETENTION_HEADS, DV).transpose(2, 0, 1, 3)
    decay_all = decay_log.reshape(RETENTION_HEADS, blocks, TOK_DEV)

    def per_head(item):

        def advance(carried, block):
            intra, query_decayed, block_state, block_total = block_pieces(*block)
            cross = jnp.dot(query_decayed, carried, precision=lax.Precision.HIGHEST, preferred_element_type=jnp.float32)
            updated = jnp.exp(block_total) * carried + block_state
            return (updated, intra + cross)
        _, retained = lax.scan(advance, jnp.zeros((DK, DV), jnp.float32), item)
        return retained.reshape(length, DV)
    retained = lax.map(per_head, (query_all, key_all, value_all, decay_all))
    normed = retained * lax.rsqrt(lax.optimization_barrier(jnp.mean(retained * retained, axis=-1, keepdims=True)) + 1e-06)
    gate_heads = gates.reshape(length, RETENTION_HEADS, DV).transpose(1, 0, 2).astype(jnp.float32)
    gated = (jax.nn.silu(gate_heads) * normed).astype(jnp.bfloat16)
    gated = gated.transpose(1, 0, 2).reshape(length, RETENTION_HEADS * DV)
    return jnp.dot(gated, out_weight, preferred_element_type=jnp.float32).astype(jnp.bfloat16)
```

```python
import jax
import jax.numpy as jnp
from jax import lax
from jax.experimental import pallas as pl
from jax.experimental.pallas import tpu as pltpu
from jax.sharding import PartitionSpec as P

MESH = pl.DeviceIdType.MESH
F32, BF16 = jnp.float32, jnp.bfloat16
SIDE = 4
BLOCK = 1024
DK, DV = 256, 512
COLS = 256
TILE = 256
TILES = BLOCK // TILE
CHUNKS = 8
ROWS = DK // CHUNKS


def dot(p, q, dims=((1,), (0,))):
    return lax.dot_general(p, q, (dims, ((), ())), preferred_element_type=F32)


def kernel(
    q_hbm, k_hbm, v_hbm, g_hbm, d_ref, w_hbm, o_ref,
    q, k, v, g, wg, col, state, carr, nxt, prob, ret, gat, part, come, own,
    ld, w_s, w_r, c_s, c_r, g_s, g_r, p_s, p_r,
):
    dp, z, tp = lax.axis_index("dp"), lax.axis_index("ctx"), lax.axis_index("tp")
    nz = lax.axis_size("ctx")
    y, x = tp // SIDE, tp % SIDE
    a = x + dp * (y - x)
    b = y + dp * (x - y)

    def place(a_, b_):
        return (1 - dp) * (SIDE * b_ + a_) + dp * (SIDE * a_ + b_)

    def a_peer(j):
        return (dp, z, place((a + j) % SIDE, b))

    def b_peer(j):
        return (dp, z, place(a, (b + j) % SIDE))

    def z_peer(j):
        return (dp, (z + j + nz) % nz, tp)

    barrier = pltpu.get_barrier_semaphore()
    for j in (1, 2, 3):
        pl.semaphore_signal(barrier, inc=1, device_id=a_peer(j), device_id_type=MESH)
        pl.semaphore_signal(barrier, inc=1, device_id=b_peer(j), device_id_type=MESH)
    for j in (1, -1):
        pl.semaphore_signal(barrier, inc=1, device_id=z_peer(j), device_id_type=MESH)

    loads = [
        pltpu.make_async_copy(src, dst, ld.at[i])
        for i, (src, dst) in enumerate(((k_hbm, k), (v_hbm, v), (q_hbm, q), (g_hbm, g)))
    ]
    for c in loads:
        c.start()
    a_rows = pl.ds(pl.multiple_of(a * DV, DV), DV)

    def w_cols(a_, c):
        return pl.ds(pl.multiple_of(place(a_, c) * COLS, COLS), COLS)

    own_w = [
        pltpu.make_async_copy(w_hbm.at[:, w_cols(a, c)], wg.at[c, a_rows], ld.at[4 + c])
        for c in range(SIDE)
    ]
    for c in own_w:
        c.start()
    pl.semaphore_wait(barrier, 8)

    def w_copy(j, c):
        return pltpu.make_async_remote_copy(
            src_ref=w_hbm.at[:, w_cols((a + j) % SIDE, c)], dst_ref=wg.at[c, a_rows],
            send_sem=w_s.at[j - 1, c], recv_sem=w_r.at[j - 1, c],
            device_id=a_peer(j), device_id_type=MESH,
        )

    for c in range(SIDE):
        for j in (2, 1, 3):
            w_copy(j, c).start()

    lane = lax.broadcasted_iota(jnp.int32, (8, 128), 1)
    run = jnp.concatenate([d_ref[:, 128 * r : 128 * (r + 1)] for r in range(8)], axis=0)
    for s in (1, 2, 4, 8, 16, 32, 64):
        run = run + jnp.where(lane >= s, pltpu.roll(run, s, 1), 0.0)
    rows, before = [], jnp.zeros((1, 1), F32)
    for r in range(8):
        rows.append(run[r : r + 1] + before)
        before = before + run[r : r + 1, 127:128]
    last = before
    turned = jnp.concatenate(rows + [jnp.zeros((120, 128), F32)], axis=0).T
    for r in range(8):
        col[128 * r : 128 * (r + 1), :] = turned[:, r : r + 1]
    cum_row = jnp.concatenate(rows, axis=1)

    loads[0].wait()
    loads[1].wait()
    weighted = (k[...].astype(F32) * jnp.exp(last - col[...])).astype(BF16)
    state[...] = dot(weighted, v[...], ((0,), (0,)))

    def c_copy(c):
        return pltpu.make_async_remote_copy(
            src_ref=nxt.at[pl.ds(c * ROWS, ROWS)], dst_ref=carr.at[pl.ds(c * ROWS, ROWS)],
            send_sem=c_s.at[c], recv_sem=c_r.at[c], device_id=z_peer(1), device_id_type=MESH,
        )

    @pl.when(z == 0)
    def _():
        nxt[...] = state[...].astype(BF16)
        for c in range(CHUNKS):
            c_copy(c).start()
        carr[...] = jnp.zeros_like(carr)

    loads[2].wait()
    t_at = lax.broadcasted_iota(jnp.int32, (TILE, TILE), 0)
    s_at = lax.broadcasted_iota(jnp.int32, (TILE, TILE), 1)
    for i in range(TILES):
        mine = slice(i * TILE, (i + 1) * TILE)
        for j in range(i + 1):
            theirs = slice(j * TILE, (j + 1) * TILE)
            spread = col[mine, :] - cum_row[:, theirs]
            if i == j:
                spread = jnp.where(t_at >= s_at, spread, -1e30)
            scores = dot(q[mine, :], k[theirs, :], ((1,), (1,)))
            prob[:, theirs] = (scores * jnp.exp(spread)).astype(BF16)
        upto = (i + 1) * TILE
        ret[mine, :] = dot(prob[:, :upto], v[:upto, :])

    @pl.when(z > 0)
    def _():
        fade = jnp.exp(last)
        for c in range(CHUNKS):
            at = slice(c * ROWS, (c + 1) * ROWS)
            c_copy(c).wait_recv()

            @pl.when(z < nz - 1)
            def _():
                nxt[at, :] = (fade * carr[at, :].astype(F32) + state[at, :]).astype(BF16)
                c_copy(c).start()

    loads[3].wait()

    def g_copy(i, j):
        here = gat.at[i, :, a_rows]
        return pltpu.make_async_remote_copy(
            src_ref=here, dst_ref=here, send_sem=g_s.at[i, j - 1], recv_sem=g_r.at[i, j - 1],
            device_id=a_peer(j), device_id_type=MESH,
        )

    def p_copy(i, j):
        return pltpu.make_async_remote_copy(
            src_ref=part.at[i, j - 1], dst_ref=come.at[i, j - 1],
            send_sem=p_s.at[i, j - 1], recv_sem=p_r.at[i, j - 1],
            device_id=b_peer(j), device_id_type=MESH,
        )

    @pl.loop(0, TILES)
    def _(i):
        at = pl.ds(pl.multiple_of(i * TILE, TILE), TILE)
        r = ret[at, :] + jnp.exp(col[at, :]) * dot(q[at, :], carr[...])
        r = r * lax.rsqrt(jnp.mean(r * r, axis=-1, keepdims=True) + 1e-6)
        u = g[at, :].astype(F32)
        gat[i, :, a_rows] = (u / (1.0 + jnp.exp(-u)) * r).astype(BF16)
        for j in (2, 1, 3):
            g_copy(i, j).start()

    for c in own_w:
        c.wait()
    for c in range(SIDE):
        for j in (1, 2, 3):
            w_copy(j, c).wait_recv()

    @pl.loop(0, TILES)
    def _(i):
        for j in (1, 2, 3):
            g_copy(i, j).wait_recv()
        heads = gat[i]
        for j in (2, 1, 3):
            part[i, j - 1] = dot(heads, wg[(b + j) % SIDE]).astype(BF16)
            p_copy(i, j).start()
        own[i] = dot(heads, wg[b])

    @pl.loop(0, TILES)
    def _(i):
        for j in (1, 2, 3):
            p_copy(i, j).wait_recv()
        total = own[i]
        for j in (1, 2, 3):
            total = total + come[i, j - 1].astype(F32)
        o_ref[pl.ds(pl.multiple_of(i * TILE, TILE), TILE), :] = total.astype(BF16)

    for c in range(SIDE):
        for j in (1, 2, 3):
            w_copy(j, c).wait_send()

    @pl.when(z < nz - 1)
    def _():
        for c in range(CHUNKS):
            c_copy(c).wait_send()

    @pl.loop(0, TILES)
    def _(i):
        for j in (1, 2, 3):
            g_copy(i, j).wait_send()
            p_copy(i, j).wait_send()


def layer(queries, keys, values, gates, decay_log, out_weight):
    dma = pltpu.SemaphoreType.DMA
    anywhere = pl.BlockSpec(memory_space=pl.ANY)
    vmem = pl.BlockSpec(memory_space=pltpu.VMEM)
    return pl.pallas_call(
        kernel,
        out_shape=jax.ShapeDtypeStruct((BLOCK, COLS), BF16),
        in_specs=[anywhere] * 4 + [vmem, anywhere],
        out_specs=vmem,
        scratch_shapes=[
            pltpu.VMEM((BLOCK, DK), BF16),
            pltpu.VMEM((BLOCK, DK), BF16),
            pltpu.VMEM((BLOCK, DV), BF16),
            pltpu.VMEM((BLOCK, DV), BF16),
            pltpu.VMEM((SIDE, SIDE * DV, COLS), BF16),
            pltpu.VMEM((BLOCK, 1), F32),
            pltpu.VMEM((DK, DV), F32),
            pltpu.VMEM((DK, DV), BF16),
            pltpu.VMEM((DK, DV), BF16),
            pltpu.VMEM((TILE, BLOCK), BF16),
            pltpu.VMEM((BLOCK, DV), F32),
            pltpu.VMEM((TILES, TILE, SIDE * DV), BF16),
            pltpu.VMEM((TILES, 3, TILE, COLS), BF16),
            pltpu.VMEM((TILES, 3, TILE, COLS), BF16),
            pltpu.VMEM((TILES, TILE, COLS), F32),
            dma((8,)),
            dma((3, SIDE)), dma((3, SIDE)),
            dma((CHUNKS,)), dma((CHUNKS,)),
            dma((TILES, 3)), dma((TILES, 3)),
            dma((TILES, 3)), dma((TILES, 3)),
        ],
        compiler_params=pltpu.CompilerParams(
            collective_id=0, has_side_effects=True, vmem_limit_bytes=48 * 2**20
        ),
        cost_estimate=pl.CostEstimate(
            flops=7 * 10**9, bytes_accessed=8 * 2**20, transcendentals=2 * 2**20
        ),
        name="retention",
    )(queries, keys, values, gates, decay_log, out_weight)


def solution(mesh):
    rows = P(("dp", "ctx"), "tp")
    placed = (rows, rows, rows, rows, P("tp", ("dp", "ctx")), P("tp", None))
    return jax.shard_map(layer, mesh=mesh, in_specs=placed, out_specs=rows, check_vma=False)
```

```python
import jax
import jax.numpy as jnp
from jax import lax
from jax.experimental import pallas as pl
from jax.experimental.pallas import tpu as pltpu
from jax.sharding import PartitionSpec as P

MESH = pl.DeviceIdType.MESH
F32, BF16 = jnp.float32, jnp.bfloat16
SIDE = 4
BLOCK = 1024
DK, DV = 256, 512
COLS = 256
TILE = 256
TILES = BLOCK // TILE
CHUNKS = 8
ROWS = DK // CHUNKS


def dot(p, q, dims=((1,), (0,))):
    return lax.dot_general(p, q, (dims, ((), ())), preferred_element_type=F32)


def kernel(
    q_hbm, k_hbm, v_hbm, g_hbm, d_ref, w_hbm, o_ref,
    q, k, v, g, wg, col, state, carr, nxt, prob, ret, gat, part, come, own,
    ld, w_s, w_r, c_s, c_r, g_s, g_r, f_s, f_r, p_s, p_r,
):
    dp, z, tp = lax.axis_index("dp"), lax.axis_index("ctx"), lax.axis_index("tp")
    nz = lax.axis_size("ctx")
    y, x = tp // SIDE, tp % SIDE
    a = x + dp * (y - x)
    b = y + dp * (x - y)

    def place(a_, b_):
        return (1 - dp) * (SIDE * b_ + a_) + dp * (SIDE * a_ + b_)

    def a_peer(j):
        return (dp, z, place((a + j) % SIDE, b))

    def b_peer(j):
        return (dp, z, place(a, (b + j) % SIDE))

    def z_peer(j):
        return (dp, (z + j + nz) % nz, tp)

    barrier = pltpu.get_barrier_semaphore()
    for j in (1, 2, 3):
        pl.semaphore_signal(barrier, inc=1, device_id=a_peer(j), device_id_type=MESH)
        pl.semaphore_signal(barrier, inc=1, device_id=b_peer(j), device_id_type=MESH)
    for j in (1, -1):
        pl.semaphore_signal(barrier, inc=1, device_id=z_peer(j), device_id_type=MESH)

    loads = [
        pltpu.make_async_copy(src, dst, ld.at[i])
        for i, (src, dst) in enumerate(((k_hbm, k), (v_hbm, v), (q_hbm, q), (g_hbm, g)))
    ]
    for c in loads:
        c.start()
    a_rows = pl.ds(pl.multiple_of(a * DV, DV), DV)

    def w_cols(a_, c):
        return pl.ds(pl.multiple_of(place(a_, c) * COLS, COLS), COLS)

    own_w = [
        pltpu.make_async_copy(w_hbm.at[:, w_cols(a, c)], wg.at[c, a_rows], ld.at[4 + c])
        for c in range(SIDE)
    ]
    for c in own_w:
        c.start()
    pl.semaphore_wait(barrier, 8)

    def w_copy(j, c):
        return pltpu.make_async_remote_copy(
            src_ref=w_hbm.at[:, w_cols((a + j) % SIDE, c)], dst_ref=wg.at[c, a_rows],
            send_sem=w_s.at[j - 1, c], recv_sem=w_r.at[j - 1, c],
            device_id=a_peer(j), device_id_type=MESH,
        )

    for c in range(SIDE):
        for j in (2, 1, 3):
            w_copy(j, c).start()

    lane = lax.broadcasted_iota(jnp.int32, (8, 128), 1)
    run = jnp.concatenate([d_ref[:, 128 * r : 128 * (r + 1)] for r in range(8)], axis=0)
    for s in (1, 2, 4, 8, 16, 32, 64):
        run = run + jnp.where(lane >= s, pltpu.roll(run, s, 1), 0.0)
    rows, before = [], jnp.zeros((1, 1), F32)
    for r in range(8):
        rows.append(run[r : r + 1] + before)
        before = before + run[r : r + 1, 127:128]
    last = before
    turned = jnp.concatenate(rows + [jnp.zeros((120, 128), F32)], axis=0).T
    for r in range(8):
        col[128 * r : 128 * (r + 1), :] = turned[:, r : r + 1]
    cum_row = jnp.concatenate(rows, axis=1)

    loads[0].wait()
    loads[1].wait()
    weighted = (k[...].astype(F32) * jnp.exp(last - col[...])).astype(BF16)
    state[...] = dot(weighted, v[...], ((0,), (0,)))

    def c_copy(c):
        return pltpu.make_async_remote_copy(
            src_ref=nxt.at[pl.ds(c * ROWS, ROWS)], dst_ref=carr.at[pl.ds(c * ROWS, ROWS)],
            send_sem=c_s.at[c], recv_sem=c_r.at[c], device_id=z_peer(1), device_id_type=MESH,
        )

    @pl.when(z == 0)
    def _():
        nxt[...] = state[...].astype(BF16)
        for c in range(CHUNKS):
            c_copy(c).start()
        carr[...] = jnp.zeros_like(carr)

    loads[2].wait()
    t_at = lax.broadcasted_iota(jnp.int32, (TILE, TILE), 0)
    s_at = lax.broadcasted_iota(jnp.int32, (TILE, TILE), 1)
    for i in range(TILES):
        mine = slice(i * TILE, (i + 1) * TILE)
        for j in range(i + 1):
            theirs = slice(j * TILE, (j + 1) * TILE)
            spread = col[mine, :] - cum_row[:, theirs]
            if i == j:
                spread = jnp.where(t_at >= s_at, spread, -1e30)
            scores = dot(q[mine, :], k[theirs, :], ((1,), (1,)))
            prob[:, theirs] = (scores * jnp.exp(spread)).astype(BF16)
        upto = (i + 1) * TILE
        ret[mine, :] = dot(prob[:, :upto], v[:upto, :])

    @pl.when(z > 0)
    def _():
        fade = jnp.exp(last)
        for c in range(CHUNKS):
            at = slice(c * ROWS, (c + 1) * ROWS)
            c_copy(c).wait_recv()

            @pl.when(z < nz - 1)
            def _():
                nxt[at, :] = (fade * carr[at, :].astype(F32) + state[at, :]).astype(BF16)
                c_copy(c).start()

    loads[3].wait()

    def g_copy(i, j):
        here = gat.at[i, :, a_rows]
        return pltpu.make_async_remote_copy(
            src_ref=here, dst_ref=here, send_sem=g_s.at[i, j // 2], recv_sem=g_r.at[i, j // 2],
            device_id=a_peer(j), device_id_type=MESH,
        )

    def f_copy(i, j):
        cols = pl.ds(pl.multiple_of((a + 4 - j) % SIDE * DV, DV), DV)
        here = gat.at[i, pl.ds(j // 2 * (TILE // 2), TILE // 2), cols]
        return pltpu.make_async_remote_copy(
            src_ref=here, dst_ref=here, send_sem=f_s.at[i, j // 2], recv_sem=f_r.at[i, j // 2],
            device_id=a_peer(j), device_id_type=MESH,
        )

    def pass_on(i):
        for j in (1, 3):
            g_copy(i, j).wait_recv()
            f_copy(i, j).start()

    def p_copy(i, j):
        return pltpu.make_async_remote_copy(
            src_ref=part.at[i, j - 1], dst_ref=come.at[i, j - 1],
            send_sem=p_s.at[i, j - 1], recv_sem=p_r.at[i, j - 1],
            device_id=b_peer(j), device_id_type=MESH,
        )

    @pl.loop(0, TILES)
    def _(i):
        at = pl.ds(pl.multiple_of(i * TILE, TILE), TILE)
        r = ret[at, :] + jnp.exp(col[at, :]) * dot(q[at, :], carr[...])
        r = r * lax.rsqrt(jnp.mean(r * r, axis=-1, keepdims=True) + 1e-6)
        u = g[at, :].astype(F32)
        gat[i, :, a_rows] = (u / (1.0 + jnp.exp(-u)) * r).astype(BF16)
        for j in (1, 3):
            g_copy(i, j).start()

    for c in own_w:
        c.wait()
    for c in range(SIDE):
        for j in (1, 2, 3):
            w_copy(j, c).wait_recv()

    pass_on(0)

    @pl.loop(0, TILES)
    def _(i):
        @pl.when(i < TILES - 1)
        def _():
            pass_on(i + 1)

        for j in (1, 3):
            f_copy(i, j).wait_recv()
        heads = gat[i]
        for j in (2, 1, 3):
            part[i, j - 1] = dot(heads, wg[(b + j) % SIDE]).astype(BF16)
            p_copy(i, j).start()
        own[i] = dot(heads, wg[b])

    @pl.loop(0, TILES)
    def _(i):
        for j in (1, 2, 3):
            p_copy(i, j).wait_recv()
        total = own[i]
        for j in (1, 2, 3):
            total = total + come[i, j - 1].astype(F32)
        o_ref[pl.ds(pl.multiple_of(i * TILE, TILE), TILE), :] = total.astype(BF16)

    for c in range(SIDE):
        for j in (1, 2, 3):
            w_copy(j, c).wait_send()

    @pl.when(z < nz - 1)
    def _():
        for c in range(CHUNKS):
            c_copy(c).wait_send()

    @pl.loop(0, TILES)
    def _(i):
        for j in (1, 3):
            g_copy(i, j).wait_send()
            f_copy(i, j).wait_send()
        for j in (1, 2, 3):
            p_copy(i, j).wait_send()


def layer(queries, keys, values, gates, decay_log, out_weight):
    dma = pltpu.SemaphoreType.DMA
    anywhere = pl.BlockSpec(memory_space=pl.ANY)
    vmem = pl.BlockSpec(memory_space=pltpu.VMEM)
    return pl.pallas_call(
        kernel,
        out_shape=jax.ShapeDtypeStruct((BLOCK, COLS), BF16),
        in_specs=[anywhere] * 4 + [vmem, anywhere],
        out_specs=vmem,
        scratch_shapes=[
            pltpu.VMEM((BLOCK, DK), BF16),
            pltpu.VMEM((BLOCK, DK), BF16),
            pltpu.VMEM((BLOCK, DV), BF16),
            pltpu.VMEM((BLOCK, DV), BF16),
            pltpu.VMEM((SIDE, SIDE * DV, COLS), BF16),
            pltpu.VMEM((BLOCK, 1), F32),
            pltpu.VMEM((DK, DV), F32),
            pltpu.VMEM((DK, DV), BF16),
            pltpu.VMEM((DK, DV), BF16),
            pltpu.VMEM((TILE, BLOCK), BF16),
            pltpu.VMEM((BLOCK, DV), F32),
            pltpu.VMEM((TILES, TILE, SIDE * DV), BF16),
            pltpu.VMEM((TILES, 3, TILE, COLS), BF16),
            pltpu.VMEM((TILES, 3, TILE, COLS), BF16),
            pltpu.VMEM((TILES, TILE, COLS), F32),
            dma((8,)),
            dma((3, SIDE)), dma((3, SIDE)),
            dma((CHUNKS,)), dma((CHUNKS,)),
            dma((TILES, 2)), dma((TILES, 2)),
            dma((TILES, 2)), dma((TILES, 2)),
            dma((TILES, 3)), dma((TILES, 3)),
        ],
        compiler_params=pltpu.CompilerParams(
            collective_id=0, has_side_effects=True, vmem_limit_bytes=60 * 2**20
        ),
        cost_estimate=pl.CostEstimate(
            flops=7 * 10**9, bytes_accessed=8 * 2**20, transcendentals=2 * 2**20
        ),
        name="retention",
    )(queries, keys, values, gates, decay_log, out_weight)


def solution(mesh):
    rows = P(("dp", "ctx"), "tp")
    placed = (rows, rows, rows, rows, P("tp", ("dp", "ctx")), P("tp", None))
    return jax.shard_map(layer, mesh=mesh, in_specs=placed, out_specs=rows, check_vma=False)
```

```python
import jax
import jax.numpy as jnp
from jax import lax
from jax.experimental import pallas as pl
from jax.experimental.pallas import tpu as pltpu
from jax.sharding import PartitionSpec as P

MESH = pl.DeviceIdType.MESH
F32, BF16 = jnp.float32, jnp.bfloat16
SIDE = 4
BLOCK = 1024
DK, DV = 256, 512
COLS = 256
TILE = 256
TILES = BLOCK // TILE
AHEAD = 2
CHUNKS = 16
ROWS = DK // CHUNKS


def dot(p, q, dims=((1,), (0,))):
    return lax.dot_general(p, q, (dims, ((), ())), preferred_element_type=F32)


def kernel(
    q_hbm, k_hbm, v_hbm, g_hbm, d_ref, w_hbm, o_ref,
    q, k, v, g, wg, col, state, into, out, tell, told, prob, ret, gat, part, come, own,
    ld, w_s, w_r, c_s, c_r, t_s, t_r, g_s, g_r, f_s, f_r, p_s, p_r,
):
    dp, z, tp = lax.axis_index("dp"), lax.axis_index("ctx"), lax.axis_index("tp")
    nz = lax.axis_size("ctx")
    y, x = tp // SIDE, tp % SIDE
    a = x + dp * (y - x)
    b = y + dp * (x - y)

    def place(a_, b_):
        return (1 - dp) * (SIDE * b_ + a_) + dp * (SIDE * a_ + b_)

    def a_peer(j):
        return (dp, z, place((a + j) % SIDE, b))

    def b_peer(j):
        return (dp, z, place(a, (b + j) % SIDE))

    def z_peer(j):
        return (dp, (z + j + nz) % nz, tp)

    barrier = pltpu.get_barrier_semaphore()
    for j in (1, 2, 3):
        pl.semaphore_signal(barrier, inc=1, device_id=a_peer(j), device_id_type=MESH)
        pl.semaphore_signal(barrier, inc=1, device_id=b_peer(j), device_id_type=MESH)
    for j in (1, -1):
        pl.semaphore_signal(barrier, inc=1, device_id=z_peer(j), device_id_type=MESH)

    loads = [
        pltpu.make_async_copy(src, dst, ld.at[i])
        for i, (src, dst) in enumerate(((k_hbm, k), (v_hbm, v), (q_hbm, q), (g_hbm, g)))
    ]
    for c in loads:
        c.start()
    a_rows = pl.ds(pl.multiple_of(a * DV, DV), DV)

    def w_cols(a_, c):
        return pl.ds(pl.multiple_of(place(a_, c) * COLS, COLS), COLS)

    own_w = [
        pltpu.make_async_copy(w_hbm.at[:, w_cols(a, c)], wg.at[c, a_rows], ld.at[4 + c])
        for c in range(SIDE)
    ]
    for c in own_w:
        c.start()
    pl.semaphore_wait(barrier, 8)

    def w_copy(j, c):
        return pltpu.make_async_remote_copy(
            src_ref=w_hbm.at[:, w_cols((a + j) % SIDE, c)], dst_ref=wg.at[c, a_rows],
            send_sem=w_s.at[j - 1, c], recv_sem=w_r.at[j - 1, c],
            device_id=a_peer(j), device_id_type=MESH,
        )

    for c in range(SIDE):
        for j in (2, 1, 3):
            w_copy(j, c).start()

    lane = lax.broadcasted_iota(jnp.int32, (8, 128), 1)
    run = jnp.concatenate([d_ref[:, 128 * r : 128 * (r + 1)] for r in range(8)], axis=0)
    for s in (1, 2, 4, 8, 16, 32, 64):
        run = run + jnp.where(lane >= s, pltpu.roll(run, s, 1), 0.0)
    rows, before = [], jnp.zeros((1, 1), F32)
    for r in range(8):
        rows.append(run[r : r + 1] + before)
        before = before + run[r : r + 1, 127:128]
    last = before
    turned = jnp.concatenate(rows + [jnp.zeros((120, 128), F32)], axis=0).T
    for r in range(8):
        col[128 * r : 128 * (r + 1), :] = turned[:, r : r + 1]
    cum_row = jnp.concatenate(rows, axis=1)

    loads[0].wait()
    loads[1].wait()
    weighted = (k[...].astype(F32) * jnp.exp(last - col[...])).astype(BF16)
    state[...] = dot(weighted, v[...], ((0,), (0,)))

    fade = jnp.exp(last)

    def chunk(c):
        return pl.ds(pl.multiple_of(c * ROWS, ROWS), ROWS)

    def c_copy(s, c, passing=False):
        src = into if passing else out
        return pltpu.make_async_remote_copy(
            src_ref=src.at[s, chunk(c)], dst_ref=into.at[s, chunk(c)],
            send_sem=c_s.at[s, c], recv_sem=c_r.at[s, c],
            device_id=z_peer(-1 if s == 2 else 1), device_id_type=MESH,
        )

    def w_tell(s):
        return pltpu.make_async_remote_copy(
            src_ref=tell.at[s], dst_ref=told.at[s], send_sem=t_s.at[s], recv_sem=t_r.at[s],
            device_id=z_peer(-1 if s == 2 else 1), device_id_type=MESH,
        )

    def source(s):
        if s:
            tell[s] = jnp.broadcast_to(fade, (8, 128))
            w_tell(s).start()
        out[s] = state[...].astype(BF16)
        for c in range(CHUNKS):
            c_copy(s, c).start()

    def relay(s):
        if s:
            w_tell(s).wait_recv()
            tell[s] = told[s] * fade

            @pl.when(z > 0)
            def _():
                w_tell(s).start()

        scale = told[2, 0:1, 0:1] if s == 2 else fade

        @pl.loop(0, CHUNKS)
        def _(c):
            c_copy(s, c).wait_recv()
            came, held = into[s, chunk(c), :].astype(F32), state[chunk(c), :]
            new = came + scale * held if s == 2 else scale * came + held
            out[s, chunk(c), :] = new.astype(BF16)
            c_copy(s, c).start()

    def accept(s):
        for c in range(CHUNKS):
            c_copy(s, c).wait_recv()

    def join():
        into[0] = (into[1].astype(F32) + told[1, 0:1, 0:1] * into[2].astype(F32)).astype(BF16)

    @pl.when(z == 0)
    def _():
        source(0)
        into[0] = jnp.zeros((DK, DV), BF16)

    @pl.when(z == 4)
    def _():
        source(1)

    @pl.when(z == 3)
    def _():
        source(2)

    loads[2].wait()
    t_at = lax.broadcasted_iota(jnp.int32, (TILE, TILE), 0)
    s_at = lax.broadcasted_iota(jnp.int32, (TILE, TILE), 1)
    for i in range(TILES):
        mine = slice(i * TILE, (i + 1) * TILE)
        for j in range(i + 1):
            theirs = slice(j * TILE, (j + 1) * TILE)
            spread = col[mine, :] - cum_row[:, theirs]
            if i == j:
                spread = jnp.where(t_at >= s_at, spread, -1e30)
            scores = dot(q[mine, :], k[theirs, :], ((1,), (1,)))
            prob[:, theirs] = (scores * jnp.exp(spread)).astype(BF16)
        upto = (i + 1) * TILE
        ret[mine, :] = dot(prob[:, :upto], v[:upto, :])

    @pl.when(z == 2)
    def _():
        relay(2)

    @pl.when((z == 5) | (z == 6))
    def _():
        relay(1)

    @pl.when((z >= 1) & (z <= 4))
    def _():
        relay(0)

    @pl.when(z <= 1)
    def _():
        relay(2)

    @pl.when(z == 5)
    def _():
        accept(0)

    @pl.when(z == 6)
    def _():
        accept(2)
        join()

    @pl.when(z == 7)
    def _():
        @pl.loop(0, CHUNKS)
        def _(c):
            c_copy(2, c).wait_recv()
            c_copy(2, c, True).start()

        w_tell(1).wait_recv()
        accept(1)
        join()

    loads[3].wait()

    def g_copy(i, j):
        here = gat.at[i, :, a_rows]
        return pltpu.make_async_remote_copy(
            src_ref=here, dst_ref=here, send_sem=g_s.at[i, j // 2], recv_sem=g_r.at[i, j // 2],
            device_id=a_peer(j), device_id_type=MESH,
        )

    def f_copy(i, j):
        cols = pl.ds(pl.multiple_of((a + 4 - j) % SIDE * DV, DV), DV)
        here = gat.at[i, pl.ds(j // 2 * (TILE // 2), TILE // 2), cols]
        return pltpu.make_async_remote_copy(
            src_ref=here, dst_ref=here, send_sem=f_s.at[i, j // 2], recv_sem=f_r.at[i, j // 2],
            device_id=a_peer(j), device_id_type=MESH,
        )

    def pass_on(i):
        for j in (1, 3):
            g_copy(i, j).wait_recv()
            f_copy(i, j).start()

    def p_copy(i, j):
        return pltpu.make_async_remote_copy(
            src_ref=part.at[i, j - 1], dst_ref=come.at[i, j - 1],
            send_sem=p_s.at[i, j - 1], recv_sem=p_r.at[i, j - 1],
            device_id=b_peer(j), device_id_type=MESH,
        )

    def gate(i):
        at = pl.ds(pl.multiple_of(i * TILE, TILE), TILE)
        r = ret[at, :] + jnp.exp(col[at, :]) * dot(q[at, :], into[0])
        r = r * lax.rsqrt(jnp.mean(r * r, axis=-1, keepdims=True) + 1e-6)
        u = g[at, :].astype(F32)
        gat[i, :, a_rows] = (u / (1.0 + jnp.exp(-u)) * r).astype(BF16)
        for j in (1, 3):
            g_copy(i, j).start()

    def project(i):
        for j in (1, 3):
            f_copy(i, j).wait_recv()
        heads = gat[i]
        for j in (2, 1, 3):
            part[i, j - 1] = dot(heads, wg[(b + j) % SIDE]).astype(BF16)
            p_copy(i, j).start()
        own[i] = dot(heads, wg[b])

    @pl.loop(0, AHEAD)
    def _(i):
        gate(i)

    @pl.loop(0, TILES + 1)
    def _(i):
        @pl.when(i < TILES)
        def _():
            pass_on(i)

        @pl.when(i + AHEAD < TILES)
        def _():
            gate(i + AHEAD)

        @pl.when(i == 1)
        def _():
            for c in own_w:
                c.wait()
            for c in range(SIDE):
                for j in (1, 2, 3):
                    w_copy(j, c).wait_recv()

        @pl.when(i > 0)
        def _():
            project(i - 1)

    @pl.loop(0, TILES)
    def _(i):
        for j in (1, 2, 3):
            p_copy(i, j).wait_recv()
        total = own[i]
        for j in (1, 2, 3):
            total = total + come[i, j - 1].astype(F32)
        o_ref[pl.ds(pl.multiple_of(i * TILE, TILE), TILE), :] = total.astype(BF16)

    for c in range(SIDE):
        for j in (1, 2, 3):
            w_copy(j, c).wait_send()

    def sent(s):
        for c in range(CHUNKS):
            c_copy(s, c).wait_send()

    @pl.when(z <= 4)
    def _():
        sent(0)

    @pl.when((z >= 4) & (z <= 6))
    def _():
        sent(1)
        w_tell(1).wait_send()

    @pl.when((z <= 3) | (z == 7))
    def _():
        sent(2)

    @pl.when((z >= 1) & (z <= 3))
    def _():
        w_tell(2).wait_send()

    @pl.loop(0, TILES)
    def _(i):
        for j in (1, 3):
            g_copy(i, j).wait_send()
            f_copy(i, j).wait_send()
        for j in (1, 2, 3):
            p_copy(i, j).wait_send()


def layer(queries, keys, values, gates, decay_log, out_weight):
    dma = pltpu.SemaphoreType.DMA
    anywhere = pl.BlockSpec(memory_space=pl.ANY)
    vmem = pl.BlockSpec(memory_space=pltpu.VMEM)
    return pl.pallas_call(
        kernel,
        out_shape=jax.ShapeDtypeStruct((BLOCK, COLS), BF16),
        in_specs=[anywhere] * 4 + [vmem, anywhere],
        out_specs=vmem,
        scratch_shapes=[
            pltpu.VMEM((BLOCK, DK), BF16),
            pltpu.VMEM((BLOCK, DK), BF16),
            pltpu.VMEM((BLOCK, DV), BF16),
            pltpu.VMEM((BLOCK, DV), BF16),
            pltpu.VMEM((SIDE, SIDE * DV, COLS), BF16),
            pltpu.VMEM((BLOCK, 1), F32),
            pltpu.VMEM((DK, DV), F32),
            pltpu.VMEM((3, DK, DV), BF16),
            pltpu.VMEM((3, DK, DV), BF16),
            pltpu.VMEM((3, 8, 128), F32),
            pltpu.VMEM((3, 8, 128), F32),
            pltpu.VMEM((TILE, BLOCK), BF16),
            pltpu.VMEM((BLOCK, DV), F32),
            pltpu.VMEM((TILES, TILE, SIDE * DV), BF16),
            pltpu.VMEM((TILES, 3, TILE, COLS), BF16),
            pltpu.VMEM((TILES, 3, TILE, COLS), BF16),
            pltpu.VMEM((TILES, TILE, COLS), F32),
            dma((8,)),
            dma((3, SIDE)), dma((3, SIDE)),
            dma((3, CHUNKS)), dma((3, CHUNKS)),
            dma((3,)), dma((3,)),
            dma((TILES, 2)), dma((TILES, 2)),
            dma((TILES, 2)), dma((TILES, 2)),
            dma((TILES, 3)), dma((TILES, 3)),
        ],
        compiler_params=pltpu.CompilerParams(
            collective_id=0, has_side_effects=True, vmem_limit_bytes=60 * 2**20
        ),
        cost_estimate=pl.CostEstimate(
            flops=7 * 10**9, bytes_accessed=8 * 2**20, transcendentals=2 * 2**20
        ),
        name="retention",
    )(queries, keys, values, gates, decay_log, out_weight)


def solution(mesh):
    rows = P(("dp", "ctx"), "tp")
    placed = (rows, rows, rows, rows, P("tp", ("dp", "ctx")), P("tp", None))
    return jax.shard_map(layer, mesh=mesh, in_specs=placed, out_specs=rows, check_vma=False)
```

```python
import jax
import jax.numpy as jnp
from jax import lax
from jax.experimental import pallas as pl
from jax.experimental.pallas import tpu as pltpu
from jax.sharding import PartitionSpec as P

MESH = pl.DeviceIdType.MESH
F32, BF16 = jnp.float32, jnp.bfloat16
SIDE = 4
BLOCK = 1024
DK, DV = 256, 512
COLS = 256
TILE = 256
TILES = BLOCK // TILE
AHEAD = 2
CHUNKS = 16
ROWS = DK // CHUNKS


def dot(p, q, dims=((1,), (0,))):
    return lax.dot_general(p, q, (dims, ((), ())), preferred_element_type=F32)


def kernel(
    q_hbm, k_hbm, v_hbm, g_hbm, d_ref, w_hbm, o_ref,
    q, k, v, g, wg, col, state, into, out, tell, told, prob, ret, gat, part, come, own,
    ld, w_s, w_r, x_s, x_r, c_s, c_r, t_s, t_r, g_s, g_r, f_s, f_r, p_s, p_r,
):
    dp, z, tp = lax.axis_index("dp"), lax.axis_index("ctx"), lax.axis_index("tp")
    nz = lax.axis_size("ctx")
    y, x = tp // SIDE, tp % SIDE
    a = x + dp * (y - x)
    b = y + dp * (x - y)

    def place(a_, b_):
        return (1 - dp) * (SIDE * b_ + a_) + dp * (SIDE * a_ + b_)

    def a_peer(j):
        return (dp, z, place((a + j) % SIDE, b))

    def b_peer(j):
        return (dp, z, place(a, (b + j) % SIDE))

    def z_peer(j):
        return (dp, (z + j + nz) % nz, tp)

    barrier = pltpu.get_barrier_semaphore()
    for j in (1, 2, 3):
        pl.semaphore_signal(barrier, inc=1, device_id=a_peer(j), device_id_type=MESH)
        pl.semaphore_signal(barrier, inc=1, device_id=b_peer(j), device_id_type=MESH)
    for j in (1, -1):
        pl.semaphore_signal(barrier, inc=1, device_id=z_peer(j), device_id_type=MESH)

    loads = [
        pltpu.make_async_copy(src, dst, ld.at[i])
        for i, (src, dst) in enumerate(((k_hbm, k), (v_hbm, v), (q_hbm, q), (g_hbm, g)))
    ]
    for c in loads:
        c.start()
    a_rows = pl.ds(pl.multiple_of(a * DV, DV), DV)

    def w_cols(a_, c):
        return pl.ds(pl.multiple_of(place(a_, c) * COLS, COLS), COLS)

    own_w = [
        pltpu.make_async_copy(w_hbm.at[:, w_cols(a, c)], wg.at[c, a_rows], ld.at[4 + c])
        for c in range(SIDE)
    ]
    for c in own_w:
        c.start()
    parity = z % 2
    order = [(j, c) for c in (0, 1) for j in (2, 1, 3)]

    def w_copy(j, c, other=False):
        c_ = 2 * (1 - parity if other else parity) + c
        return pltpu.make_async_remote_copy(
            src_ref=w_hbm.at[:, w_cols((a + j) % SIDE, c_)], dst_ref=wg.at[c_, a_rows],
            send_sem=w_s.at[int(other), j - 1, c], recv_sem=w_r.at[int(other), j - 1, c],
            device_id=a_peer(j), device_id_type=MESH,
        )

    def x_copy(u, j, c, coming=False):
        c_ = 2 * (1 - parity if coming else parity) + c
        half = (a + SIDE - j) % SIDE * DV + u * (DV // 2)
        here = wg.at[c_, pl.ds(pl.multiple_of(half, DV // 2), DV // 2)]
        return pltpu.make_async_remote_copy(
            src_ref=here, dst_ref=here, send_sem=x_s.at[u, j - 1, c], recv_sem=x_r.at[u, j - 1, c],
            device_id=z_peer(1 - 2 * u), device_id_type=MESH,
        )

    def share(halves):
        for j, c in order:
            w_copy(j, c).wait_recv()
            for u in halves:
                x_copy(u, j, c).start()

    lane = lax.broadcasted_iota(jnp.int32, (8, 128), 1)
    run = jnp.concatenate([d_ref[:, 128 * r : 128 * (r + 1)] for r in range(8)], axis=0)
    for s in (1, 2, 4, 8, 16, 32, 64):
        run = run + jnp.where(lane >= s, pltpu.roll(run, s, 1), 0.0)
    rows, before = [], jnp.zeros((1, 1), F32)
    for r in range(8):
        rows.append(run[r : r + 1] + before)
        before = before + run[r : r + 1, 127:128]
    last = before
    turned = jnp.concatenate(rows + [jnp.zeros((120, 128), F32)], axis=0).T
    for r in range(8):
        col[128 * r : 128 * (r + 1), :] = turned[:, r : r + 1]
    cum_row = jnp.concatenate(rows, axis=1)

    loads[0].wait()
    loads[1].wait()
    weighted = (k[...].astype(F32) * jnp.exp(last - col[...])).astype(BF16)
    state[...] = dot(weighted, v[...], ((0,), (0,)))

    fade = jnp.exp(last)

    def chunk(c):
        return pl.ds(pl.multiple_of(c * ROWS, ROWS), ROWS)

    def c_copy(s, c, passing=False):
        src = into if passing else out
        return pltpu.make_async_remote_copy(
            src_ref=src.at[s, chunk(c)], dst_ref=into.at[s, chunk(c)],
            send_sem=c_s.at[s, c], recv_sem=c_r.at[s, c],
            device_id=z_peer(-1 if s == 2 else 1), device_id_type=MESH,
        )

    def w_tell(s):
        return pltpu.make_async_remote_copy(
            src_ref=tell.at[s], dst_ref=told.at[s], send_sem=t_s.at[s], recv_sem=t_r.at[s],
            device_id=z_peer(-1 if s == 2 else 1), device_id_type=MESH,
        )

    def source(s):
        if s:
            tell[s] = jnp.broadcast_to(fade, (8, 128))
            w_tell(s).start()
        out[s] = state[...].astype(BF16)
        for c in range(CHUNKS):
            c_copy(s, c).start()

    def relay(s):
        if s:
            w_tell(s).wait_recv()
            tell[s] = told[s] * fade

            @pl.when(z > 0)
            def _():
                w_tell(s).start()

        scale = told[2, 0:1, 0:1] if s == 2 else fade

        @pl.loop(0, CHUNKS)
        def _(c):
            c_copy(s, c).wait_recv()
            came, held = into[s, chunk(c), :].astype(F32), state[chunk(c), :]
            new = came + scale * held if s == 2 else scale * came + held
            out[s, chunk(c), :] = new.astype(BF16)
            c_copy(s, c).start()

    def accept(s):
        for c in range(CHUNKS):
            c_copy(s, c).wait_recv()

    def join():
        into[0] = (into[1].astype(F32) + told[1, 0:1, 0:1] * into[2].astype(F32)).astype(BF16)

    pl.semaphore_wait(barrier, 8)

    @pl.when(z == 0)
    def _():
        source(0)
        into[0] = jnp.zeros((DK, DV), BF16)

    @pl.when(z == 4)
    def _():
        source(1)

    @pl.when(z == 3)
    def _():
        source(2)

    for j, c in order:
        w_copy(j, c).start()

    @pl.when(z >= 4)
    def _():
        for j, c in order:
            w_copy(j, c, True).start()

    loads[2].wait()
    t_at = lax.broadcasted_iota(jnp.int32, (TILE, TILE), 0)
    s_at = lax.broadcasted_iota(jnp.int32, (TILE, TILE), 1)
    for i in range(TILES):
        mine = slice(i * TILE, (i + 1) * TILE)
        for j in range(i + 1):
            theirs = slice(j * TILE, (j + 1) * TILE)
            spread = col[mine, :] - cum_row[:, theirs]
            if i == j:
                spread = jnp.where(t_at >= s_at, spread, -1e30)
            scores = dot(q[mine, :], k[theirs, :], ((1,), (1,)))
            prob[:, theirs] = (scores * jnp.exp(spread)).astype(BF16)
        upto = (i + 1) * TILE
        ret[mine, :] = dot(prob[:, :upto], v[:upto, :])

    loads[3].wait()

    def g_copy(i, j):
        here = gat.at[i, :, a_rows]
        return pltpu.make_async_remote_copy(
            src_ref=here, dst_ref=here, send_sem=g_s.at[i, j // 2], recv_sem=g_r.at[i, j // 2],
            device_id=a_peer(j), device_id_type=MESH,
        )

    def f_copy(i, j):
        cols = pl.ds(pl.multiple_of((a + 4 - j) % SIDE * DV, DV), DV)
        here = gat.at[i, pl.ds(j // 2 * (TILE // 2), TILE // 2), cols]
        return pltpu.make_async_remote_copy(
            src_ref=here, dst_ref=here, send_sem=f_s.at[i, j // 2], recv_sem=f_r.at[i, j // 2],
            device_id=a_peer(j), device_id_type=MESH,
        )

    def pass_on(i):
        for j in (1, 3):
            g_copy(i, j).wait_recv()
            f_copy(i, j).start()

    def gate(i):
        at = pl.ds(pl.multiple_of(i * TILE, TILE), TILE)
        r = ret[at, :] + jnp.exp(col[at, :]) * dot(q[at, :], into[0])
        r = r * lax.rsqrt(jnp.mean(r * r, axis=-1, keepdims=True) + 1e-6)
        u = g[at, :].astype(F32)
        gat[i, :, a_rows] = (u / (1.0 + jnp.exp(-u)) * r).astype(BF16)
        for j in (1, 3):
            g_copy(i, j).start()

    def start_gates():
        @pl.loop(0, AHEAD)
        def _(i):
            gate(i)

    @pl.when(z == 2)
    def _():
        relay(2)

    @pl.when((z == 5) | (z == 6))
    def _():
        relay(1)

    @pl.when(z == 0)
    def _():
        start_gates()

    @pl.when(z == 7)
    def _():
        share((0,))

    @pl.when((z >= 1) & (z <= 4))
    def _():
        relay(0)

    @pl.when(z <= 1)
    def _():
        relay(2)

    @pl.when(z == 0)
    def _():
        share((0,))

    @pl.when((z == 1) | (z == 2))
    def _():
        share((0, 1))

    @pl.when((z == 3) | (z == 4))
    def _():
        share((1,))

    @pl.when(z == 5)
    def _():
        accept(0)

    @pl.when(z == 6)
    def _():
        accept(2)
        join()

    @pl.when(z == 7)
    def _():
        @pl.loop(0, CHUNKS)
        def _(c):
            c_copy(2, c).wait_recv()
            c_copy(2, c, True).start()

        w_tell(1).wait_recv()
        accept(1)
        join()

    def p_copy(i, j):
        return pltpu.make_async_remote_copy(
            src_ref=part.at[i, j - 1], dst_ref=come.at[i, j - 1],
            send_sem=p_s.at[i, j - 1], recv_sem=p_r.at[i, j - 1],
            device_id=b_peer(j), device_id_type=MESH,
        )

    def project(i):
        for j in (1, 3):
            f_copy(i, j).wait_recv()
        heads = gat[i]
        for j in (2, 1, 3):
            part[i, j - 1] = dot(heads, wg[(b + j) % SIDE]).astype(BF16)
            p_copy(i, j).start()
        own[i] = dot(heads, wg[b])

    @pl.when(z > 0)
    def _():
        start_gates()

    @pl.loop(0, TILES + 1)
    def _(i):
        @pl.when(i < TILES)
        def _():
            pass_on(i)

        @pl.when(i + AHEAD < TILES)
        def _():
            gate(i + AHEAD)

        @pl.when(i == 1)
        def _():
            for c in own_w:
                c.wait()

            @pl.when(z < 4)
            def _():
                for j, c in order:
                    for u in (0, 1):
                        x_copy(u, j, c, True).wait_recv()

            @pl.when((z == 5) | (z == 6))
            def _():
                share(())

            @pl.when(z >= 4)
            def _():
                for j, c in order:
                    w_copy(j, c, True).wait_recv()

        @pl.when(i > 0)
        def _():
            project(i - 1)

    @pl.loop(0, TILES)
    def _(i):
        for j in (1, 2, 3):
            p_copy(i, j).wait_recv()
        total = own[i]
        for j in (1, 2, 3):
            total = total + come[i, j - 1].astype(F32)
        o_ref[pl.ds(pl.multiple_of(i * TILE, TILE), TILE), :] = total.astype(BF16)

    def shared(u):
        for j, c in order:
            x_copy(u, j, c).wait_send()

    for j, c in order:
        w_copy(j, c).wait_send()

    @pl.when(z >= 4)
    def _():
        for j, c in order:
            w_copy(j, c, True).wait_send()

    @pl.when((z <= 2) | (z == 7))
    def _():
        shared(0)

    @pl.when((z >= 1) & (z <= 4))
    def _():
        shared(1)

    def sent(s):
        for c in range(CHUNKS):
            c_copy(s, c).wait_send()

    @pl.when(z <= 4)
    def _():
        sent(0)

    @pl.when((z >= 4) & (z <= 6))
    def _():
        sent(1)
        w_tell(1).wait_send()

    @pl.when((z <= 3) | (z == 7))
    def _():
        sent(2)

    @pl.when((z >= 1) & (z <= 3))
    def _():
        w_tell(2).wait_send()

    @pl.loop(0, TILES)
    def _(i):
        for j in (1, 3):
            g_copy(i, j).wait_send()
            f_copy(i, j).wait_send()
        for j in (1, 2, 3):
            p_copy(i, j).wait_send()


def layer(queries, keys, values, gates, decay_log, out_weight):
    dma = pltpu.SemaphoreType.DMA
    hbm = pl.BlockSpec(memory_space=pltpu.HBM)
    vmem = pl.BlockSpec(memory_space=pltpu.VMEM)
    return pl.pallas_call(
        kernel,
        out_shape=jax.ShapeDtypeStruct((BLOCK, COLS), BF16),
        in_specs=[hbm] * 4 + [vmem, hbm],
        out_specs=vmem,
        scratch_shapes=[
            pltpu.VMEM((BLOCK, DK), BF16),
            pltpu.VMEM((BLOCK, DK), BF16),
            pltpu.VMEM((BLOCK, DV), BF16),
            pltpu.VMEM((BLOCK, DV), BF16),
            pltpu.VMEM((SIDE, SIDE * DV, COLS), BF16),
            pltpu.VMEM((BLOCK, 1), F32),
            pltpu.VMEM((DK, DV), F32),
            pltpu.VMEM((3, DK, DV), BF16),
            pltpu.VMEM((3, DK, DV), BF16),
            pltpu.VMEM((3, 8, 128), F32),
            pltpu.VMEM((3, 8, 128), F32),
            pltpu.VMEM((TILE, BLOCK), BF16),
            pltpu.VMEM((BLOCK, DV), F32),
            pltpu.VMEM((TILES, TILE, SIDE * DV), BF16),
            pltpu.VMEM((TILES, 3, TILE, COLS), BF16),
            pltpu.VMEM((TILES, 3, TILE, COLS), BF16),
            pltpu.VMEM((TILES, TILE, COLS), F32),
            dma((8,)),
            dma((2, 3, 2)), dma((2, 3, 2)),
            dma((2, 3, 2)), dma((2, 3, 2)),
            dma((3, CHUNKS)), dma((3, CHUNKS)),
            dma((3,)), dma((3,)),
            dma((TILES, 2)), dma((TILES, 2)),
            dma((TILES, 2)), dma((TILES, 2)),
            dma((TILES, 3)), dma((TILES, 3)),
        ],
        compiler_params=pltpu.CompilerParams(
            collective_id=0, has_side_effects=True, vmem_limit_bytes=53 * 2**20
        ),
        cost_estimate=pl.CostEstimate(
            flops=7 * 10**9, bytes_accessed=8 * 2**20, transcendentals=2 * 2**20
        ),
        name="retention",
    )(queries, keys, values, gates, decay_log, out_weight)


def solution(mesh):
    rows = P(("dp", "ctx"), "tp")
    placed = (rows, rows, rows, rows, P("tp", ("dp", "ctx")), P("tp", None))
    return jax.shard_map(layer, mesh=mesh, in_specs=placed, out_specs=rows, check_vma=False)
```

```python
import jax
import jax.numpy as jnp
from jax import lax
from jax.experimental import pallas as pl
from jax.experimental.pallas import tpu as pltpu
from jax.sharding import PartitionSpec as P

MESH = pl.DeviceIdType.MESH
F32, BF16 = jnp.float32, jnp.bfloat16
SIDE = 4
BLOCK = 1024
DK, DV = 256, 512
COLS = 256
TILE = 256
TILES = BLOCK // TILE
SPAN = 256
SPANS = BLOCK // SPAN
AHEAD = 3
LAG = 3
CHUNKS = 16
ROWS = DK // CHUNKS


def dot(p, q, dims=((1,), (0,))):
    return lax.dot_general(p, q, (dims, ((), ())), preferred_element_type=F32)


def kernel(
    q_hbm, k_hbm, v_hbm, g_hbm, d_ref, w_hbm, o_ref,
    q, k, v, g, wg, col, state, into, out, tell, told, prob, ret, gat, part, come, own,
    ld, w_s, w_r, x_s, x_r, c_s, c_r, t_s, t_r, g_s, g_r, f_s, f_r, p_s, p_r,
):
    dp, z, tp = lax.axis_index("dp"), lax.axis_index("ctx"), lax.axis_index("tp")
    nz = lax.axis_size("ctx")
    y, x = tp // SIDE, tp % SIDE
    a = x + dp * (y - x)
    b = y + dp * (x - y)

    def place(a_, b_):
        return (1 - dp) * (SIDE * b_ + a_) + dp * (SIDE * a_ + b_)

    def a_peer(j):
        return (dp, z, place((a + j) % SIDE, b))

    def b_peer(j):
        return (dp, z, place(a, (b + j) % SIDE))

    def z_peer(j):
        return (dp, (z + j + nz) % nz, tp)

    barrier = pltpu.get_barrier_semaphore()
    for j in (1, 2, 3):
        pl.semaphore_signal(barrier, inc=1, device_id=a_peer(j), device_id_type=MESH)
        pl.semaphore_signal(barrier, inc=1, device_id=b_peer(j), device_id_type=MESH)
    for j in (1, -1):
        pl.semaphore_signal(barrier, inc=1, device_id=z_peer(j), device_id_type=MESH)

    loads = [
        pltpu.make_async_copy(src, dst, ld.at[i])
        for i, (src, dst) in enumerate(((k_hbm, k), (v_hbm, v), (q_hbm, q), (g_hbm, g)))
    ]
    for c in loads[:2]:
        c.start()
    a_rows = pl.ds(pl.multiple_of(a * DV, DV), DV)

    def w_cols(a_, c):
        return pl.ds(pl.multiple_of(place(a_, c) * COLS, COLS), COLS)

    own_w = [
        pltpu.make_async_copy(w_hbm.at[:, w_cols(a, c)], wg.at[c, a_rows], ld.at[4 + c])
        for c in range(SIDE)
    ]
    parity = z % 2
    order = [(j, c) for c in (0, 1) for j in (2, 1, 3)]

    def w_copy(j, c, other=False):
        c_ = 2 * (1 - parity if other else parity) + c
        return pltpu.make_async_remote_copy(
            src_ref=w_hbm.at[:, w_cols((a + j) % SIDE, c_)], dst_ref=wg.at[c_, a_rows],
            send_sem=w_s.at[int(other), j - 1, c], recv_sem=w_r.at[int(other), j - 1, c],
            device_id=a_peer(j), device_id_type=MESH,
        )

    def x_copy(u, j, c, coming=False):
        c_ = 2 * (1 - parity if coming else parity) + c
        half = (a + SIDE - j) % SIDE * DV + u * (DV // 2)
        here = wg.at[c_, pl.ds(pl.multiple_of(half, DV // 2), DV // 2)]
        return pltpu.make_async_remote_copy(
            src_ref=here, dst_ref=here, send_sem=x_s.at[u, j - 1, c], recv_sem=x_r.at[u, j - 1, c],
            device_id=z_peer(1 - 2 * u), device_id_type=MESH,
        )

    def share(halves):
        for j, c in order:
            w_copy(j, c).wait_recv()
            for u in halves:
                x_copy(u, j, c).start()

    lane = lax.broadcasted_iota(jnp.int32, (8, 128), 1)
    run = jnp.concatenate([d_ref[:, 128 * r : 128 * (r + 1)] for r in range(8)], axis=0)
    for s in (1, 2, 4, 8, 16, 32, 64):
        run = run + jnp.where(lane >= s, pltpu.roll(run, s, 1), 0.0)
    rows, before = [], jnp.zeros((1, 1), F32)
    for r in range(8):
        rows.append(run[r : r + 1] + before)
        before = before + run[r : r + 1, 127:128]
    last = before
    turned = jnp.concatenate(rows + [jnp.zeros((120, 128), F32)], axis=0).T
    for r in range(8):
        col[128 * r : 128 * (r + 1), :] = turned[:, r : r + 1]
    cum_row = jnp.concatenate(rows, axis=1)

    loads[0].wait()
    loads[1].wait()
    loads[2].start()
    weighted = (k[...].astype(F32) * jnp.exp(last - col[...])).astype(BF16)
    state[...] = dot(weighted, v[...], ((0,), (0,)))

    fade = jnp.exp(last)

    def chunk(c):
        return pl.ds(pl.multiple_of(c * ROWS, ROWS), ROWS)

    def c_copy(s, c, passing=False):
        src = into if passing else out
        return pltpu.make_async_remote_copy(
            src_ref=src.at[s, chunk(c)], dst_ref=into.at[s, chunk(c)],
            send_sem=c_s.at[s, c], recv_sem=c_r.at[s, c],
            device_id=z_peer(-1 if s == 2 else 1), device_id_type=MESH,
        )

    def w_tell(s):
        return pltpu.make_async_remote_copy(
            src_ref=tell.at[s], dst_ref=told.at[s], send_sem=t_s.at[s], recv_sem=t_r.at[s],
            device_id=z_peer(-1 if s == 2 else 1), device_id_type=MESH,
        )

    def source(s):
        if s:
            tell[s] = jnp.broadcast_to(fade, (8, 128))
            w_tell(s).start()
        out[s] = state[...].astype(BF16)
        for c in range(CHUNKS):
            c_copy(s, c).start()

    def relay(s):
        if s:
            w_tell(s).wait_recv()
            tell[s] = told[s] * fade

            @pl.when(z > 0)
            def _():
                w_tell(s).start()

        scale = told[2, 0:1, 0:1] if s == 2 else fade

        @pl.loop(0, CHUNKS)
        def _(c):
            c_copy(s, c).wait_recv()
            came, held = into[s, chunk(c), :].astype(F32), state[chunk(c), :]
            new = came + scale * held if s == 2 else scale * came + held
            out[s, chunk(c), :] = new.astype(BF16)
            c_copy(s, c).start()

    def accept(s):
        for c in range(CHUNKS):
            c_copy(s, c).wait_recv()

    def join():
        into[0] = (into[1].astype(F32) + told[1, 0:1, 0:1] * into[2].astype(F32)).astype(BF16)

    pl.semaphore_wait(barrier, 8)

    @pl.when(z == 0)
    def _():
        source(0)
        into[0] = jnp.zeros((DK, DV), BF16)

    @pl.when(z == 4)
    def _():
        source(1)

    @pl.when(z == 3)
    def _():
        source(2)

    for j, c in order:
        w_copy(j, c).start()

    @pl.when(z >= 4)
    def _():
        for j, c in order:
            w_copy(j, c, True).start()

    loads[3].start()
    for c in own_w:
        c.start()
    loads[2].wait()
    t_at = lax.broadcasted_iota(jnp.int32, (SPAN, SPAN), 0)
    s_at = lax.broadcasted_iota(jnp.int32, (SPAN, SPAN), 1)
    for i in range(SPANS):
        mine = slice(i * SPAN, (i + 1) * SPAN)
        for j in range(i + 1):
            theirs = slice(j * SPAN, (j + 1) * SPAN)
            spread = col[mine, :] - cum_row[:, theirs]
            if i == j:
                spread = jnp.where(t_at >= s_at, spread, -1e30)
            scores = dot(q[mine, :], k[theirs, :], ((1,), (1,)))
            prob[:, theirs] = (scores * jnp.exp(spread)).astype(BF16)
        upto = (i + 1) * SPAN
        ret[mine, :] = dot(prob[:, :upto], v[:upto, :])

    loads[3].wait()

    def g_copy(i, j):
        here = gat.at[i, :, a_rows]
        return pltpu.make_async_remote_copy(
            src_ref=here, dst_ref=here, send_sem=g_s.at[i, j // 2], recv_sem=g_r.at[i, j // 2],
            device_id=a_peer(j), device_id_type=MESH,
        )

    def f_copy(i, j):
        cols = pl.ds(pl.multiple_of((a + 4 - j) % SIDE * DV, DV), DV)
        here = gat.at[i, pl.ds(j // 2 * (TILE // 2), TILE // 2), cols]
        return pltpu.make_async_remote_copy(
            src_ref=here, dst_ref=here, send_sem=f_s.at[i, j // 2], recv_sem=f_r.at[i, j // 2],
            device_id=a_peer(j), device_id_type=MESH,
        )

    def pass_on(i):
        for j in (1, 3):
            g_copy(i, j).wait_recv()
            f_copy(i, j).start()

    def gate(i):
        at = pl.ds(pl.multiple_of(i * TILE, TILE), TILE)
        r = ret[at, :] + jnp.exp(col[at, :]) * dot(q[at, :], into[0])
        r = r * lax.rsqrt(jnp.mean(r * r, axis=-1, keepdims=True) + 1e-6)
        u = g[at, :].astype(F32)
        gat[i, :, a_rows] = (u / (1.0 + jnp.exp(-u)) * r).astype(BF16)
        for j in (1, 3):
            g_copy(i, j).start()

    def start_gates():
        @pl.loop(0, AHEAD)
        def _(i):
            gate(i)

    @pl.when(z == 2)
    def _():
        relay(2)

    @pl.when((z == 5) | (z == 6))
    def _():
        relay(1)

    @pl.when(z == 0)
    def _():
        start_gates()

    @pl.when(z == 7)
    def _():
        share((0,))

    @pl.when((z >= 1) & (z <= 4))
    def _():
        relay(0)

    @pl.when(z <= 1)
    def _():
        relay(2)

    @pl.when(z == 0)
    def _():
        share((0,))

    @pl.when((z == 1) | (z == 2))
    def _():
        share((0, 1))

    @pl.when((z == 3) | (z == 4))
    def _():
        share((1,))

    @pl.when(z == 5)
    def _():
        accept(0)

    @pl.when(z == 6)
    def _():
        accept(2)
        join()

    @pl.when(z == 7)
    def _():
        @pl.loop(0, CHUNKS)
        def _(c):
            c_copy(2, c).wait_recv()
            c_copy(2, c, True).start()

        w_tell(1).wait_recv()
        accept(1)
        join()

    def p_copy(i, j):
        return pltpu.make_async_remote_copy(
            src_ref=part.at[i, j - 1], dst_ref=come.at[i, j - 1],
            send_sem=p_s.at[i, j - 1], recv_sem=p_r.at[i, j - 1],
            device_id=b_peer(j), device_id_type=MESH,
        )

    def project(i):
        for j in (1, 3):
            f_copy(i, j).wait_recv()
        heads = gat[i]
        for j in (2, 1, 3):
            part[i, j - 1] = dot(heads, wg[(b + j) % SIDE]).astype(BF16)
            p_copy(i, j).start()
        own[i] = dot(heads, wg[b])

    @pl.when(z > 0)
    def _():
        start_gates()

    @pl.loop(0, TILES + LAG)
    def _(i):
        @pl.when(i < TILES)
        def _():
            pass_on(i)

        @pl.when(i + AHEAD < TILES)
        def _():
            gate(i + AHEAD)

        @pl.when(i == LAG)
        def _():
            for c in own_w:
                c.wait()

            @pl.when(z < 4)
            def _():
                for j, c in order:
                    for u in (0, 1):
                        x_copy(u, j, c, True).wait_recv()

            @pl.when((z == 5) | (z == 6))
            def _():
                share(())

            @pl.when(z >= 4)
            def _():
                for j, c in order:
                    w_copy(j, c, True).wait_recv()

        @pl.when(i >= LAG)
        def _():
            project(i - LAG)

    @pl.loop(0, TILES)
    def _(i):
        for j in (1, 2, 3):
            p_copy(i, j).wait_recv()
        total = own[i]
        for j in (1, 2, 3):
            total = total + come[i, j - 1].astype(F32)
        o_ref[pl.ds(pl.multiple_of(i * TILE, TILE), TILE), :] = total.astype(BF16)

    def shared(u):
        for j, c in order:
            x_copy(u, j, c).wait_send()

    for j, c in order:
        w_copy(j, c).wait_send()

    @pl.when(z >= 4)
    def _():
        for j, c in order:
            w_copy(j, c, True).wait_send()

    @pl.when((z <= 2) | (z == 7))
    def _():
        shared(0)

    @pl.when((z >= 1) & (z <= 4))
    def _():
        shared(1)

    def sent(s):
        for c in range(CHUNKS):
            c_copy(s, c).wait_send()

    @pl.when(z <= 4)
    def _():
        sent(0)

    @pl.when((z >= 4) & (z <= 6))
    def _():
        sent(1)
        w_tell(1).wait_send()

    @pl.when((z <= 3) | (z == 7))
    def _():
        sent(2)

    @pl.when((z >= 1) & (z <= 3))
    def _():
        w_tell(2).wait_send()

    @pl.loop(0, TILES)
    def _(i):
        for j in (1, 3):
            g_copy(i, j).wait_send()
            f_copy(i, j).wait_send()
        for j in (1, 2, 3):
            p_copy(i, j).wait_send()


def layer(queries, keys, values, gates, decay_log, out_weight):
    dma = pltpu.SemaphoreType.DMA
    hbm = pl.BlockSpec(memory_space=pltpu.HBM)
    vmem = pl.BlockSpec(memory_space=pltpu.VMEM)
    return pl.pallas_call(
        kernel,
        out_shape=jax.ShapeDtypeStruct((BLOCK, COLS), BF16),
        in_specs=[hbm] * 4 + [vmem, hbm],
        out_specs=vmem,
        scratch_shapes=[
            pltpu.VMEM((BLOCK, DK), BF16),
            pltpu.VMEM((BLOCK, DK), BF16),
            pltpu.VMEM((BLOCK, DV), BF16),
            pltpu.VMEM((BLOCK, DV), BF16),
            pltpu.VMEM((SIDE, SIDE * DV, COLS), BF16),
            pltpu.VMEM((BLOCK, 1), F32),
            pltpu.VMEM((DK, DV), F32),
            pltpu.VMEM((3, DK, DV), BF16),
            pltpu.VMEM((3, DK, DV), BF16),
            pltpu.VMEM((3, 8, 128), F32),
            pltpu.VMEM((3, 8, 128), F32),
            pltpu.VMEM((SPAN, BLOCK), BF16),
            pltpu.VMEM((BLOCK, DV), F32),
            pltpu.VMEM((TILES, TILE, SIDE * DV), BF16),
            pltpu.VMEM((TILES, 3, TILE, COLS), BF16),
            pltpu.VMEM((TILES, 3, TILE, COLS), BF16),
            pltpu.VMEM((TILES, TILE, COLS), F32),
            dma((8,)),
            dma((2, 3, 2)), dma((2, 3, 2)),
            dma((2, 3, 2)), dma((2, 3, 2)),
            dma((3, CHUNKS)), dma((3, CHUNKS)),
            dma((3,)), dma((3,)),
            dma((TILES, 2)), dma((TILES, 2)),
            dma((TILES, 2)), dma((TILES, 2)),
            dma((TILES, 3)), dma((TILES, 3)),
        ],
        compiler_params=pltpu.CompilerParams(
            collective_id=0, has_side_effects=True, vmem_limit_bytes=53 * 2**20
        ),
        cost_estimate=pl.CostEstimate(
            flops=7 * 10**9, bytes_accessed=8 * 2**20, transcendentals=2 * 2**20
        ),
        name="retention",
    )(queries, keys, values, gates, decay_log, out_weight)


def solution(mesh):
    rows = P(("dp", "ctx"), "tp")
    placed = (rows, rows, rows, rows, P("tp", ("dp", "ctx")), P("tp", None))
    return jax.shard_map(layer, mesh=mesh, in_specs=placed, out_specs=rows, check_vma=False)
```

```python
import jax
import jax.numpy as jnp
from jax import lax
from jax.experimental import pallas as pl
from jax.experimental.pallas import tpu as pltpu
from jax.sharding import PartitionSpec as P

MESH = pl.DeviceIdType.MESH
F32, BF16 = jnp.float32, jnp.bfloat16
SIDE = 4
BLOCK = 1024
DK, DV = 256, 512
COLS = 256
TILE = 256
TILES = BLOCK // TILE
SPAN = 256
SPANS = BLOCK // SPAN
AHEAD = 3
LAG = 3
CHUNKS = 16
ROWS = DK // CHUNKS


def dot(p, q, dims=((1,), (0,))):
    return lax.dot_general(p, q, (dims, ((), ())), preferred_element_type=F32)


def kernel(
    q_hbm, k_hbm, v_hbm, g_hbm, d_ref, w_hbm, o_ref,
    q, k, v, g, wg, col, state, into, out, tell, told, prob, ret, gat, part, come, own,
    ld, w_s, w_r, x_s, x_r, c_s, c_r, t_s, t_r, g_s, g_r, f_s, f_r, p_s, p_r,
):
    dp, z, tp = lax.axis_index("dp"), lax.axis_index("ctx"), lax.axis_index("tp")
    nz = lax.axis_size("ctx")
    y, x = tp // SIDE, tp % SIDE
    a = x + dp * (y - x)
    b = y + dp * (x - y)

    def place(a_, b_):
        return (1 - dp) * (SIDE * b_ + a_) + dp * (SIDE * a_ + b_)

    def a_peer(j):
        return (dp, z, place((a + j) % SIDE, b))

    def b_peer(j):
        return (dp, z, place(a, (b + j) % SIDE))

    def z_peer(j):
        return (dp, (z + j + nz) % nz, tp)

    barrier = pltpu.get_barrier_semaphore()
    for j in (1, 2, 3):
        pl.semaphore_signal(barrier, inc=1, device_id=a_peer(j), device_id_type=MESH)
        pl.semaphore_signal(barrier, inc=1, device_id=b_peer(j), device_id_type=MESH)
    for j in (1, -1):
        pl.semaphore_signal(barrier, inc=1, device_id=z_peer(j), device_id_type=MESH)

    loads = [
        pltpu.make_async_copy(src, dst, ld.at[i])
        for i, (src, dst) in enumerate(((k_hbm, k), (v_hbm, v), (q_hbm, q), (g_hbm, g)))
    ]
    for c in loads[:2]:
        c.start()
    a_rows = pl.ds(pl.multiple_of(a * DV, DV), DV)

    def w_cols(a_, c):
        return pl.ds(pl.multiple_of(place(a_, c) * COLS, COLS), COLS)

    own_w = [
        pltpu.make_async_copy(w_hbm.at[:, w_cols(a, c)], wg.at[c, a_rows], ld.at[4 + c])
        for c in range(SIDE)
    ]
    parity = z % 2
    order = [(j, c) for c in (0, 1) for j in (2, 1, 3)]

    def w_copy(j, c, other=False):
        c_ = 2 * (1 - parity if other else parity) + c
        return pltpu.make_async_remote_copy(
            src_ref=w_hbm.at[:, w_cols((a + j) % SIDE, c_)], dst_ref=wg.at[c_, a_rows],
            send_sem=w_s.at[int(other), j - 1, c], recv_sem=w_r.at[int(other), j - 1, c],
            device_id=a_peer(j), device_id_type=MESH,
        )

    def x_copy(u, j, c, coming=False):
        c_ = 2 * (1 - parity if coming else parity) + c
        half = (a + SIDE - j) % SIDE * DV + u * (DV // 2)
        here = wg.at[c_, pl.ds(pl.multiple_of(half, DV // 2), DV // 2)]
        return pltpu.make_async_remote_copy(
            src_ref=here, dst_ref=here, send_sem=x_s.at[u, j - 1, c], recv_sem=x_r.at[u, j - 1, c],
            device_id=z_peer(1 - 2 * u), device_id_type=MESH,
        )

    def share(halves):
        for j, c in order:
            w_copy(j, c).wait_recv()
            for u in halves:
                x_copy(u, j, c).start()

    @pl.when(z >= 4)
    def _():
        pl.semaphore_wait(barrier, 8)
        for other in (False, True):
            for j, c in order:
                w_copy(j, c, other).start()

    lane = lax.broadcasted_iota(jnp.int32, (8, 128), 1)
    run = jnp.concatenate([d_ref[:, 128 * r : 128 * (r + 1)] for r in range(8)], axis=0)
    for s in (1, 2, 4, 8, 16, 32, 64):
        run = run + jnp.where(lane >= s, pltpu.roll(run, s, 1), 0.0)
    rows, before = [], jnp.zeros((1, 1), F32)
    for r in range(8):
        rows.append(run[r : r + 1] + before)
        before = before + run[r : r + 1, 127:128]
    last = before
    turned = jnp.concatenate(rows + [jnp.zeros((120, 128), F32)], axis=0).T
    for r in range(8):
        col[128 * r : 128 * (r + 1), :] = turned[:, r : r + 1]
    cum_row = jnp.concatenate(rows, axis=1)

    loads[0].wait()
    loads[1].wait()
    loads[2].start()
    weighted = (k[...].astype(F32) * jnp.exp(last - col[...])).astype(BF16)
    state[...] = dot(weighted, v[...], ((0,), (0,)))

    fade = jnp.exp(last)

    def chunk(c):
        return pl.ds(pl.multiple_of(c * ROWS, ROWS), ROWS)

    def c_copy(s, c, passing=False):
        src = into if passing else out
        return pltpu.make_async_remote_copy(
            src_ref=src.at[s, chunk(c)], dst_ref=into.at[s, chunk(c)],
            send_sem=c_s.at[s, c], recv_sem=c_r.at[s, c],
            device_id=z_peer(-1 if s == 2 else 1), device_id_type=MESH,
        )

    def w_tell(s):
        return pltpu.make_async_remote_copy(
            src_ref=tell.at[s], dst_ref=told.at[s], send_sem=t_s.at[s], recv_sem=t_r.at[s],
            device_id=z_peer(-1 if s == 2 else 1), device_id_type=MESH,
        )

    def source(s):
        if s:
            tell[s] = jnp.broadcast_to(fade, (8, 128))
            w_tell(s).start()
        out[s] = state[...].astype(BF16)
        for c in range(CHUNKS):
            c_copy(s, c).start()

    def relay(s):
        if s:
            w_tell(s).wait_recv()
            tell[s] = told[s] * fade

            @pl.when(z > 0)
            def _():
                w_tell(s).start()

        scale = told[2, 0:1, 0:1] if s == 2 else fade

        @pl.loop(0, CHUNKS)
        def _(c):
            c_copy(s, c).wait_recv()
            came, held = into[s, chunk(c), :].astype(F32), state[chunk(c), :]
            new = came + scale * held if s == 2 else scale * came + held
            out[s, chunk(c), :] = new.astype(BF16)
            c_copy(s, c).start()

    def accept(s):
        for c in range(CHUNKS):
            c_copy(s, c).wait_recv()

    def join():
        into[0] = (into[1].astype(F32) + told[1, 0:1, 0:1] * into[2].astype(F32)).astype(BF16)

    @pl.when(z < 4)
    def _():
        pl.semaphore_wait(barrier, 8)

    @pl.when(z == 0)
    def _():
        source(0)
        into[0] = jnp.zeros((DK, DV), BF16)

    @pl.when(z == 4)
    def _():
        source(1)

    @pl.when(z == 3)
    def _():
        source(2)

    @pl.when(z < 4)
    def _():
        for j, c in order:
            w_copy(j, c).start()

    loads[3].start()
    for c in own_w:
        c.start()
    loads[2].wait()
    t_at = lax.broadcasted_iota(jnp.int32, (SPAN, SPAN), 0)
    s_at = lax.broadcasted_iota(jnp.int32, (SPAN, SPAN), 1)
    for i in range(SPANS):
        mine = slice(i * SPAN, (i + 1) * SPAN)
        for j in range(i + 1):
            theirs = slice(j * SPAN, (j + 1) * SPAN)
            spread = col[mine, :] - cum_row[:, theirs]
            if i == j:
                spread = jnp.where(t_at >= s_at, spread, -1e30)
            scores = dot(q[mine, :], k[theirs, :], ((1,), (1,)))
            prob[:, theirs] = (scores * jnp.exp(spread)).astype(BF16)
        upto = (i + 1) * SPAN
        ret[mine, :] = dot(prob[:, :upto], v[:upto, :])

    loads[3].wait()

    def g_copy(i, j):
        here = gat.at[i, :, a_rows]
        return pltpu.make_async_remote_copy(
            src_ref=here, dst_ref=here, send_sem=g_s.at[i, j // 2], recv_sem=g_r.at[i, j // 2],
            device_id=a_peer(j), device_id_type=MESH,
        )

    def f_copy(i, j):
        cols = pl.ds(pl.multiple_of((a + 4 - j) % SIDE * DV, DV), DV)
        here = gat.at[i, pl.ds(j // 2 * (TILE // 2), TILE // 2), cols]
        return pltpu.make_async_remote_copy(
            src_ref=here, dst_ref=here, send_sem=f_s.at[i, j // 2], recv_sem=f_r.at[i, j // 2],
            device_id=a_peer(j), device_id_type=MESH,
        )

    def pass_on(i):
        for j in (1, 3):
            g_copy(i, j).wait_recv()
            f_copy(i, j).start()

    def gate(i):
        at = pl.ds(pl.multiple_of(i * TILE, TILE), TILE)
        r = ret[at, :] + jnp.exp(col[at, :]) * dot(q[at, :], into[0])
        r = r * lax.rsqrt(jnp.mean(r * r, axis=-1, keepdims=True) + 1e-6)
        u = g[at, :].astype(F32)
        gat[i, :, a_rows] = (u / (1.0 + jnp.exp(-u)) * r).astype(BF16)
        for j in (1, 3):
            g_copy(i, j).start()

    def start_gates():
        @pl.loop(0, AHEAD)
        def _(i):
            gate(i)

    @pl.when(z == 2)
    def _():
        relay(2)

    @pl.when((z == 5) | (z == 6))
    def _():
        relay(1)

    @pl.when(z == 0)
    def _():
        start_gates()

    @pl.when(z == 7)
    def _():
        share((0,))

    @pl.when((z >= 1) & (z <= 4))
    def _():
        relay(0)

    @pl.when(z <= 1)
    def _():
        relay(2)

    @pl.when(z == 0)
    def _():
        share((0,))

    @pl.when((z == 1) | (z == 2))
    def _():
        share((0, 1))

    @pl.when((z == 3) | (z == 4))
    def _():
        share((1,))

    @pl.when(z == 5)
    def _():
        accept(0)

    @pl.when(z == 6)
    def _():
        accept(2)
        join()

    @pl.when(z == 7)
    def _():
        @pl.loop(0, CHUNKS)
        def _(c):
            c_copy(2, c).wait_recv()
            c_copy(2, c, True).start()

        w_tell(1).wait_recv()
        accept(1)
        join()

    def p_copy(i, j):
        return pltpu.make_async_remote_copy(
            src_ref=part.at[i, j - 1], dst_ref=come.at[i, j - 1],
            send_sem=p_s.at[i, j - 1], recv_sem=p_r.at[i, j - 1],
            device_id=b_peer(j), device_id_type=MESH,
        )

    def project(i):
        for j in (1, 3):
            f_copy(i, j).wait_recv()
        heads = gat[i]
        for j in (2, 1, 3):
            part[i, j - 1] = dot(heads, wg[(b + j) % SIDE]).astype(BF16)
            p_copy(i, j).start()
        own[i] = dot(heads, wg[b])

    @pl.when(z > 0)
    def _():
        start_gates()

    @pl.loop(0, TILES + LAG)
    def _(i):
        @pl.when(i < TILES)
        def _():
            pass_on(i)

        @pl.when(i + AHEAD < TILES)
        def _():
            gate(i + AHEAD)

        @pl.when(i == LAG)
        def _():
            for c in own_w:
                c.wait()

            @pl.when(z < 4)
            def _():
                for j, c in order:
                    for u in (0, 1):
                        x_copy(u, j, c, True).wait_recv()

            @pl.when((z == 5) | (z == 6))
            def _():
                share(())

            @pl.when(z >= 4)
            def _():
                for j, c in order:
                    w_copy(j, c, True).wait_recv()

        @pl.when(i >= LAG)
        def _():
            project(i - LAG)

    @pl.loop(0, TILES)
    def _(i):
        for j in (1, 2, 3):
            p_copy(i, j).wait_recv()
        total = own[i]
        for j in (1, 2, 3):
            total = total + come[i, j - 1].astype(F32)
        o_ref[pl.ds(pl.multiple_of(i * TILE, TILE), TILE), :] = total.astype(BF16)

    def shared(u):
        for j, c in order:
            x_copy(u, j, c).wait_send()

    for j, c in order:
        w_copy(j, c).wait_send()

    @pl.when(z >= 4)
    def _():
        for j, c in order:
            w_copy(j, c, True).wait_send()

    @pl.when((z <= 2) | (z == 7))
    def _():
        shared(0)

    @pl.when((z >= 1) & (z <= 4))
    def _():
        shared(1)

    def sent(s):
        for c in range(CHUNKS):
            c_copy(s, c).wait_send()

    @pl.when(z <= 4)
    def _():
        sent(0)

    @pl.when((z >= 4) & (z <= 6))
    def _():
        sent(1)
        w_tell(1).wait_send()

    @pl.when((z <= 3) | (z == 7))
    def _():
        sent(2)

    @pl.when((z >= 1) & (z <= 3))
    def _():
        w_tell(2).wait_send()

    @pl.loop(0, TILES)
    def _(i):
        for j in (1, 3):
            g_copy(i, j).wait_send()
            f_copy(i, j).wait_send()
        for j in (1, 2, 3):
            p_copy(i, j).wait_send()


def layer(queries, keys, values, gates, decay_log, out_weight):
    dma = pltpu.SemaphoreType.DMA
    hbm = pl.BlockSpec(memory_space=pltpu.HBM)
    vmem = pl.BlockSpec(memory_space=pltpu.VMEM)
    return pl.pallas_call(
        kernel,
        out_shape=jax.ShapeDtypeStruct((BLOCK, COLS), BF16),
        in_specs=[hbm] * 4 + [vmem, hbm],
        out_specs=vmem,
        scratch_shapes=[
            pltpu.VMEM((BLOCK, DK), BF16),
            pltpu.VMEM((BLOCK, DK), BF16),
            pltpu.VMEM((BLOCK, DV), BF16),
            pltpu.VMEM((BLOCK, DV), BF16),
            pltpu.VMEM((SIDE, SIDE * DV, COLS), BF16),
            pltpu.VMEM((BLOCK, 1), F32),
            pltpu.VMEM((DK, DV), F32),
            pltpu.VMEM((3, DK, DV), BF16),
            pltpu.VMEM((3, DK, DV), BF16),
            pltpu.VMEM((3, 8, 128), F32),
            pltpu.VMEM((3, 8, 128), F32),
            pltpu.VMEM((SPAN, BLOCK), BF16),
            pltpu.VMEM((BLOCK, DV), F32),
            pltpu.VMEM((TILES, TILE, SIDE * DV), BF16),
            pltpu.VMEM((TILES, 3, TILE, COLS), BF16),
            pltpu.VMEM((TILES, 3, TILE, COLS), BF16),
            pltpu.VMEM((TILES, TILE, COLS), F32),
            dma((8,)),
            dma((2, 3, 2)), dma((2, 3, 2)),
            dma((2, 3, 2)), dma((2, 3, 2)),
            dma((3, CHUNKS)), dma((3, CHUNKS)),
            dma((3,)), dma((3,)),
            dma((TILES, 2)), dma((TILES, 2)),
            dma((TILES, 2)), dma((TILES, 2)),
            dma((TILES, 3)), dma((TILES, 3)),
        ],
        compiler_params=pltpu.CompilerParams(
            collective_id=0, has_side_effects=True, vmem_limit_bytes=53 * 2**20
        ),
        cost_estimate=pl.CostEstimate(
            flops=7 * 10**9, bytes_accessed=8 * 2**20, transcendentals=2 * 2**20
        ),
        name="retention",
    )(queries, keys, values, gates, decay_log, out_weight)


def solution(mesh):
    rows = P(("dp", "ctx"), "tp")
    placed = (rows, rows, rows, rows, P("tp", ("dp", "ctx")), P("tp", None))
    return jax.shard_map(layer, mesh=mesh, in_specs=placed, out_specs=rows, check_vma=False)
```

```python
import jax
import jax.numpy as jnp
from jax import lax
from jax.experimental import pallas as pl
from jax.experimental.pallas import tpu as pltpu
from jax.sharding import PartitionSpec as P

MESH = pl.DeviceIdType.MESH
F32, BF16 = jnp.float32, jnp.bfloat16
SIDE = 4
BLOCK = 1024
DK, DV = 256, 512
COLS = 256
TILE = 256
TILES = BLOCK // TILE
SPAN = 256
SPANS = BLOCK // SPAN
AHEAD = 3
LAG = 3
CHUNKS = 8
ROWS = DK // CHUNKS


def dot(p, q, dims=((1,), (0,))):
    return lax.dot_general(p, q, (dims, ((), ())), preferred_element_type=F32)


def kernel(
    q_hbm, k_hbm, v_hbm, g_hbm, d_ref, w_hbm, o_ref,
    q, k, v, g, wg, col, state, into, out, tell, told, prob, ret, gat, part, come, own,
    ld, w_s, w_r, x_s, x_r, c_s, c_r, t_s, t_r, g_s, g_r, f_s, f_r, p_s, p_r,
):
    dp, z, tp = lax.axis_index("dp"), lax.axis_index("ctx"), lax.axis_index("tp")
    nz = lax.axis_size("ctx")
    y, x = tp // SIDE, tp % SIDE
    a = x + dp * (y - x)
    b = y + dp * (x - y)

    def place(a_, b_):
        return (1 - dp) * (SIDE * b_ + a_) + dp * (SIDE * a_ + b_)

    def a_peer(j):
        return (dp, z, place((a + j) % SIDE, b))

    def b_peer(j):
        return (dp, z, place(a, (b + j) % SIDE))

    def z_peer(j):
        return (dp, (z + j + nz) % nz, tp)

    barrier = pltpu.get_barrier_semaphore()
    for j in (1, 2, 3):
        pl.semaphore_signal(barrier, inc=1, device_id=a_peer(j), device_id_type=MESH)
        pl.semaphore_signal(barrier, inc=1, device_id=b_peer(j), device_id_type=MESH)
    for j in (1, -1):
        pl.semaphore_signal(barrier, inc=1, device_id=z_peer(j), device_id_type=MESH)

    loads = [
        pltpu.make_async_copy(src, dst, ld.at[i])
        for i, (src, dst) in enumerate(((k_hbm, k), (v_hbm, v), (q_hbm, q), (g_hbm, g)))
    ]
    for c in loads[:2]:
        c.start()
    a_rows = pl.ds(pl.multiple_of(a * DV, DV), DV)

    def w_cols(a_, c):
        return pl.ds(pl.multiple_of(place(a_, c) * COLS, COLS), COLS)

    own_w = [
        pltpu.make_async_copy(w_hbm.at[:, w_cols(a, c)], wg.at[c, a_rows], ld.at[4 + c])
        for c in range(SIDE)
    ]
    parity = z % 2
    order = [(j, c) for c in (0, 1) for j in (2, 1, 3)]

    def w_copy(j, c, other=False):
        c_ = 2 * (1 - parity if other else parity) + c
        return pltpu.make_async_remote_copy(
            src_ref=w_hbm.at[:, w_cols((a + j) % SIDE, c_)], dst_ref=wg.at[c_, a_rows],
            send_sem=w_s.at[int(other), j - 1, c], recv_sem=w_r.at[int(other), j - 1, c],
            device_id=a_peer(j), device_id_type=MESH,
        )

    def x_copy(u, j, c, coming=False):
        c_ = 2 * (1 - parity if coming else parity) + c
        half = (a + SIDE - j) % SIDE * DV + u * (DV // 2)
        here = wg.at[c_, pl.ds(pl.multiple_of(half, DV // 2), DV // 2)]
        return pltpu.make_async_remote_copy(
            src_ref=here, dst_ref=here, send_sem=x_s.at[u, j - 1, c], recv_sem=x_r.at[u, j - 1, c],
            device_id=z_peer(1 - 2 * u), device_id_type=MESH,
        )

    def share(halves):
        for j, c in order:
            w_copy(j, c).wait_recv()
            for u in halves:
                x_copy(u, j, c).start()

    @pl.when(z >= 4)
    def _():
        pl.semaphore_wait(barrier, 8)
        for other in (False, True):
            for j, c in order:
                w_copy(j, c, other).start()

    lane = lax.broadcasted_iota(jnp.int32, (8, 128), 1)
    run = jnp.concatenate([d_ref[:, 128 * r : 128 * (r + 1)] for r in range(8)], axis=0)
    for s in (1, 2, 4, 8, 16, 32, 64):
        run = run + jnp.where(lane >= s, pltpu.roll(run, s, 1), 0.0)
    rows, before = [], jnp.zeros((1, 1), F32)
    for r in range(8):
        rows.append(run[r : r + 1] + before)
        before = before + run[r : r + 1, 127:128]
    last = before
    turned = jnp.concatenate(rows + [jnp.zeros((120, 128), F32)], axis=0).T
    for r in range(8):
        col[128 * r : 128 * (r + 1), :] = turned[:, r : r + 1]
    cum_row = jnp.concatenate(rows, axis=1)

    loads[0].wait()
    loads[1].wait()
    loads[2].start()
    weighted = (k[...].astype(F32) * jnp.exp(last - col[...])).astype(BF16)
    state[...] = dot(weighted, v[...], ((0,), (0,)))

    fade = jnp.exp(last)

    def chunk(c):
        return pl.ds(pl.multiple_of(c * ROWS, ROWS), ROWS)

    def c_copy(s, c, passing=False):
        src = into if passing else out
        return pltpu.make_async_remote_copy(
            src_ref=src.at[s, chunk(c)], dst_ref=into.at[s, chunk(c)],
            send_sem=c_s.at[s, c], recv_sem=c_r.at[s, c],
            device_id=z_peer(-1 if s == 2 else 1), device_id_type=MESH,
        )

    def w_tell(s):
        return pltpu.make_async_remote_copy(
            src_ref=tell.at[s], dst_ref=told.at[s], send_sem=t_s.at[s], recv_sem=t_r.at[s],
            device_id=z_peer(-1 if s == 2 else 1), device_id_type=MESH,
        )

    def source(s):
        if s:
            tell[s] = jnp.broadcast_to(fade, (8, 128))
            w_tell(s).start()
        out[s] = state[...].astype(BF16)
        for c in range(CHUNKS):
            c_copy(s, c).start()

    def relay(s):
        if s:
            w_tell(s).wait_recv()
            tell[s] = told[s] * fade

            @pl.when(z > 0)
            def _():
                w_tell(s).start()

        scale = told[2, 0:1, 0:1] if s == 2 else fade

        @pl.loop(0, CHUNKS)
        def _(c):
            c_copy(s, c).wait_recv()
            came, held = into[s, chunk(c), :].astype(F32), state[chunk(c), :]
            new = came + scale * held if s == 2 else scale * came + held
            out[s, chunk(c), :] = new.astype(BF16)
            c_copy(s, c).start()

    def accept(s):
        for c in range(CHUNKS):
            c_copy(s, c).wait_recv()

    def join():
        into[0] = (into[1].astype(F32) + told[1, 0:1, 0:1] * into[2].astype(F32)).astype(BF16)

    @pl.when(z < 4)
    def _():
        pl.semaphore_wait(barrier, 8)

    @pl.when(z == 0)
    def _():
        source(0)
        into[0] = jnp.zeros((DK, DV), BF16)

    @pl.when(z == 4)
    def _():
        source(1)

    @pl.when(z == 3)
    def _():
        source(2)

    @pl.when(z < 4)
    def _():
        for j, c in order:
            w_copy(j, c).start()

    loads[3].start()
    for c in own_w:
        c.start()
    loads[2].wait()
    t_at = lax.broadcasted_iota(jnp.int32, (SPAN, SPAN), 0)
    s_at = lax.broadcasted_iota(jnp.int32, (SPAN, SPAN), 1)
    for i in range(SPANS):
        mine = slice(i * SPAN, (i + 1) * SPAN)
        for j in range(i + 1):
            theirs = slice(j * SPAN, (j + 1) * SPAN)
            spread = col[mine, :] - cum_row[:, theirs]
            if i == j:
                spread = jnp.where(t_at >= s_at, spread, -1e30)
            scores = dot(q[mine, :], k[theirs, :], ((1,), (1,)))
            prob[:, theirs] = (scores * jnp.exp(spread)).astype(BF16)
        upto = (i + 1) * SPAN
        ret[mine, :] = dot(prob[:, :upto], v[:upto, :])

    loads[3].wait()

    def g_copy(i, j):
        here = gat.at[i, :, a_rows]
        return pltpu.make_async_remote_copy(
            src_ref=here, dst_ref=here, send_sem=g_s.at[i, j // 2], recv_sem=g_r.at[i, j // 2],
            device_id=a_peer(j), device_id_type=MESH,
        )

    def f_copy(i, j):
        cols = pl.ds(pl.multiple_of((a + 4 - j) % SIDE * DV, DV), DV)
        here = gat.at[i, pl.ds(j // 2 * (TILE // 2), TILE // 2), cols]
        return pltpu.make_async_remote_copy(
            src_ref=here, dst_ref=here, send_sem=f_s.at[i, j // 2], recv_sem=f_r.at[i, j // 2],
            device_id=a_peer(j), device_id_type=MESH,
        )

    def pass_on(i):
        for j in (1, 3):
            g_copy(i, j).wait_recv()
            f_copy(i, j).start()

    def gate(i):
        at = pl.ds(pl.multiple_of(i * TILE, TILE), TILE)
        r = ret[at, :] + jnp.exp(col[at, :]) * dot(q[at, :], into[0])
        r = r * lax.rsqrt(jnp.mean(r * r, axis=-1, keepdims=True) + 1e-6)
        u = g[at, :].astype(F32)
        gat[i, :, a_rows] = (u / (1.0 + jnp.exp(-u)) * r).astype(BF16)
        for j in (1, 3):
            g_copy(i, j).start()

    def start_gates():
        @pl.loop(0, AHEAD)
        def _(i):
            gate(i)

    @pl.when(z == 2)
    def _():
        relay(2)

    @pl.when((z == 5) | (z == 6))
    def _():
        relay(1)

    @pl.when(z == 0)
    def _():
        start_gates()

    @pl.when(z == 7)
    def _():
        share((0,))

    @pl.when((z >= 1) & (z <= 4))
    def _():
        relay(0)

    @pl.when(z <= 1)
    def _():
        relay(2)

    @pl.when(z == 0)
    def _():
        share((0,))

    @pl.when((z == 1) | (z == 2))
    def _():
        share((0, 1))

    @pl.when((z == 3) | (z == 4))
    def _():
        share((1,))

    @pl.when(z == 5)
    def _():
        accept(0)

    @pl.when(z == 6)
    def _():
        accept(2)
        join()

    @pl.when(z == 7)
    def _():
        @pl.loop(0, CHUNKS)
        def _(c):
            c_copy(2, c).wait_recv()
            c_copy(2, c, True).start()

        w_tell(1).wait_recv()
        accept(1)
        join()

    def p_copy(i, j):
        return pltpu.make_async_remote_copy(
            src_ref=part.at[i, j - 1], dst_ref=come.at[i, j - 1],
            send_sem=p_s.at[i, j - 1], recv_sem=p_r.at[i, j - 1],
            device_id=b_peer(j), device_id_type=MESH,
        )

    def project(i):
        for j in (1, 3):
            f_copy(i, j).wait_recv()
        heads = gat[i]
        for j in (2, 1, 3):
            part[i, j - 1] = dot(heads, wg[(b + j) % SIDE]).astype(BF16)
            p_copy(i, j).start()
        own[i] = dot(heads, wg[b])

    @pl.when(z > 0)
    def _():
        start_gates()

    @pl.loop(0, TILES + LAG)
    def _(i):
        @pl.when(i < TILES)
        def _():
            pass_on(i)

        @pl.when(i + AHEAD < TILES)
        def _():
            gate(i + AHEAD)

        @pl.when(i == LAG)
        def _():
            for c in own_w:
                c.wait()

            @pl.when(z < 4)
            def _():
                for j, c in order:
                    for u in (0, 1):
                        x_copy(u, j, c, True).wait_recv()

            @pl.when((z == 5) | (z == 6))
            def _():
                share(())

            @pl.when(z >= 4)
            def _():
                for j, c in order:
                    w_copy(j, c, True).wait_recv()

        @pl.when(i >= LAG)
        def _():
            project(i - LAG)

    @pl.loop(0, TILES)
    def _(i):
        for j in (1, 2, 3):
            p_copy(i, j).wait_recv()
        total = own[i]
        for j in (1, 2, 3):
            total = total + come[i, j - 1].astype(F32)
        o_ref[pl.ds(pl.multiple_of(i * TILE, TILE), TILE), :] = total.astype(BF16)

    def shared(u):
        for j, c in order:
            x_copy(u, j, c).wait_send()

    for j, c in order:
        w_copy(j, c).wait_send()

    @pl.when(z >= 4)
    def _():
        for j, c in order:
            w_copy(j, c, True).wait_send()

    @pl.when((z <= 2) | (z == 7))
    def _():
        shared(0)

    @pl.when((z >= 1) & (z <= 4))
    def _():
        shared(1)

    def sent(s):
        for c in range(CHUNKS):
            c_copy(s, c).wait_send()

    @pl.when(z <= 4)
    def _():
        sent(0)

    @pl.when((z >= 4) & (z <= 6))
    def _():
        sent(1)
        w_tell(1).wait_send()

    @pl.when((z <= 3) | (z == 7))
    def _():
        sent(2)

    @pl.when((z >= 1) & (z <= 3))
    def _():
        w_tell(2).wait_send()

    @pl.loop(0, TILES)
    def _(i):
        for j in (1, 3):
            g_copy(i, j).wait_send()
            f_copy(i, j).wait_send()
        for j in (1, 2, 3):
            p_copy(i, j).wait_send()


def layer(queries, keys, values, gates, decay_log, out_weight):
    dma = pltpu.SemaphoreType.DMA
    hbm = pl.BlockSpec(memory_space=pltpu.HBM)
    vmem = pl.BlockSpec(memory_space=pltpu.VMEM)
    return pl.pallas_call(
        kernel,
        out_shape=jax.ShapeDtypeStruct((BLOCK, COLS), BF16),
        in_specs=[hbm] * 4 + [vmem, hbm],
        out_specs=vmem,
        scratch_shapes=[
            pltpu.VMEM((BLOCK, DK), BF16),
            pltpu.VMEM((BLOCK, DK), BF16),
            pltpu.VMEM((BLOCK, DV), BF16),
            pltpu.VMEM((BLOCK, DV), BF16),
            pltpu.VMEM((SIDE, SIDE * DV, COLS), BF16),
            pltpu.VMEM((BLOCK, 1), F32),
            pltpu.VMEM((DK, DV), F32),
            pltpu.VMEM((3, DK, DV), BF16),
            pltpu.VMEM((3, DK, DV), BF16),
            pltpu.VMEM((3, 8, 128), F32),
            pltpu.VMEM((3, 8, 128), F32),
            pltpu.VMEM((SPAN, BLOCK), BF16),
            pltpu.VMEM((BLOCK, DV), F32),
            pltpu.VMEM((TILES, TILE, SIDE * DV), BF16),
            pltpu.VMEM((TILES, 3, TILE, COLS), BF16),
            pltpu.VMEM((TILES, 3, TILE, COLS), BF16),
            pltpu.VMEM((TILES, TILE, COLS), F32),
            dma((8,)),
            dma((2, 3, 2)), dma((2, 3, 2)),
            dma((2, 3, 2)), dma((2, 3, 2)),
            dma((3, CHUNKS)), dma((3, CHUNKS)),
            dma((3,)), dma((3,)),
            dma((TILES, 2)), dma((TILES, 2)),
            dma((TILES, 2)), dma((TILES, 2)),
            dma((TILES, 3)), dma((TILES, 3)),
        ],
        compiler_params=pltpu.CompilerParams(
            collective_id=0, has_side_effects=True, vmem_limit_bytes=53 * 2**20
        ),
        cost_estimate=pl.CostEstimate(
            flops=7 * 10**9, bytes_accessed=8 * 2**20, transcendentals=2 * 2**20
        ),
        name="retention",
    )(queries, keys, values, gates, decay_log, out_weight)


def solution(mesh):
    rows = P(("dp", "ctx"), "tp")
    placed = (rows, rows, rows, rows, P("tp", ("dp", "ctx")), P("tp", None))
    return jax.shard_map(layer, mesh=mesh, in_specs=placed, out_specs=rows, check_vma=False)
```

```python
import jax
import jax.numpy as jnp
from jax import lax
from jax.experimental import pallas as pl
from jax.experimental.pallas import tpu as pltpu
from jax.sharding import PartitionSpec as P

MESH = pl.DeviceIdType.MESH
F32, BF16 = jnp.float32, jnp.bfloat16
SIDE = 4
BLOCK = 1024
DK, DV = 256, 512
COLS = 256
TILE = 256
TILES = BLOCK // TILE
SPAN = 256
SPANS = BLOCK // SPAN
AHEAD = 4
LAG = 4
CHUNKS = 8
ROWS = DK // CHUNKS


def dot(p, q, dims=((1,), (0,))):
    return lax.dot_general(p, q, (dims, ((), ())), preferred_element_type=F32)


def kernel(
    q_hbm, k_hbm, v_hbm, g_hbm, d_ref, w_hbm, o_ref,
    q, k, v, g, wg, col, state, into, out, tell, told, prob, ret, gat, part, come, own,
    ld, w_s, w_r, x_s, x_r, c_s, c_r, t_s, t_r, g_s, g_r, f_s, f_r, p_s, p_r,
):
    dp, z, tp = lax.axis_index("dp"), lax.axis_index("ctx"), lax.axis_index("tp")
    nz = lax.axis_size("ctx")
    y, x = tp // SIDE, tp % SIDE
    a = x + dp * (y - x)
    b = y + dp * (x - y)

    def place(a_, b_):
        return (1 - dp) * (SIDE * b_ + a_) + dp * (SIDE * a_ + b_)

    def a_peer(j):
        return (dp, z, place((a + j) % SIDE, b))

    def b_peer(j):
        return (dp, z, place(a, (b + j) % SIDE))

    def z_peer(j):
        return (dp, (z + j + nz) % nz, tp)

    barrier = pltpu.get_barrier_semaphore()
    for j in (1, 2, 3):
        pl.semaphore_signal(barrier, inc=1, device_id=a_peer(j), device_id_type=MESH)
        pl.semaphore_signal(barrier, inc=1, device_id=b_peer(j), device_id_type=MESH)
    for j in (1, -1):
        pl.semaphore_signal(barrier, inc=1, device_id=z_peer(j), device_id_type=MESH)

    loads = [
        pltpu.make_async_copy(src, dst, ld.at[i])
        for i, (src, dst) in enumerate(((k_hbm, k), (v_hbm, v), (q_hbm, q), (g_hbm, g)))
    ]
    for c in loads[:2]:
        c.start()
    a_rows = pl.ds(pl.multiple_of(a * DV, DV), DV)

    def w_cols(a_, c):
        return pl.ds(pl.multiple_of(place(a_, c) * COLS, COLS), COLS)

    own_w = [
        pltpu.make_async_copy(w_hbm.at[:, w_cols(a, c)], wg.at[c, a_rows], ld.at[4 + c])
        for c in range(SIDE)
    ]
    parity = z % 2
    order = [(j, c) for c in (0, 1) for j in (2, 1, 3)]

    def w_copy(j, c, other=False):
        c_ = 2 * (1 - parity if other else parity) + c
        return pltpu.make_async_remote_copy(
            src_ref=w_hbm.at[:, w_cols((a + j) % SIDE, c_)], dst_ref=wg.at[c_, a_rows],
            send_sem=w_s.at[int(other), j - 1, c], recv_sem=w_r.at[int(other), j - 1, c],
            device_id=a_peer(j), device_id_type=MESH,
        )

    def x_copy(u, j, c, coming=False):
        c_ = 2 * (1 - parity if coming else parity) + c
        half = (a + SIDE - j) % SIDE * DV + u * (DV // 2)
        here = wg.at[c_, pl.ds(pl.multiple_of(half, DV // 2), DV // 2)]
        return pltpu.make_async_remote_copy(
            src_ref=here, dst_ref=here, send_sem=x_s.at[u, j - 1, c], recv_sem=x_r.at[u, j - 1, c],
            device_id=z_peer(1 - 2 * u), device_id_type=MESH,
        )

    def share(halves):
        for j, c in order:
            w_copy(j, c).wait_recv()
            for u in halves:
                x_copy(u, j, c).start()

    @pl.when(z >= 4)
    def _():
        pl.semaphore_wait(barrier, 8)
        for other in (False, True):
            for j, c in order:
                w_copy(j, c, other).start()

    lane = lax.broadcasted_iota(jnp.int32, (8, 128), 1)
    run = jnp.concatenate([d_ref[:, 128 * r : 128 * (r + 1)] for r in range(8)], axis=0)
    for s in (1, 2, 4, 8, 16, 32, 64):
        run = run + jnp.where(lane >= s, pltpu.roll(run, s, 1), 0.0)
    rows, before = [], jnp.zeros((1, 1), F32)
    for r in range(8):
        rows.append(run[r : r + 1] + before)
        before = before + run[r : r + 1, 127:128]
    last = before
    turned = jnp.concatenate(rows + [jnp.zeros((120, 128), F32)], axis=0).T
    for r in range(8):
        col[128 * r : 128 * (r + 1), :] = turned[:, r : r + 1]
    cum_row = jnp.concatenate(rows, axis=1)

    loads[0].wait()
    loads[1].wait()
    loads[2].start()
    weighted = (k[...].astype(F32) * jnp.exp(last - col[...])).astype(BF16)
    state[...] = dot(weighted, v[...], ((0,), (0,)))

    fade = jnp.exp(last)

    def chunk(c):
        return pl.ds(pl.multiple_of(c * ROWS, ROWS), ROWS)

    def c_copy(s, c, passing=False):
        src = into if passing else out
        return pltpu.make_async_remote_copy(
            src_ref=src.at[s, chunk(c)], dst_ref=into.at[s, chunk(c)],
            send_sem=c_s.at[s, c], recv_sem=c_r.at[s, c],
            device_id=z_peer(-1 if s == 2 else 1), device_id_type=MESH,
        )

    def w_tell(s):
        return pltpu.make_async_remote_copy(
            src_ref=tell.at[s], dst_ref=told.at[s], send_sem=t_s.at[s], recv_sem=t_r.at[s],
            device_id=z_peer(-1 if s == 2 else 1), device_id_type=MESH,
        )

    def source(s):
        if s:
            tell[s] = jnp.broadcast_to(fade, (8, 128))
            w_tell(s).start()
        out[s] = state[...].astype(BF16)
        for c in range(CHUNKS):
            c_copy(s, c).start()

    def relay(s):
        if s:
            w_tell(s).wait_recv()
            tell[s] = told[s] * fade

            @pl.when(z > 0)
            def _():
                w_tell(s).start()

        scale = told[2, 0:1, 0:1] if s == 2 else fade

        @pl.loop(0, CHUNKS)
        def _(c):
            c_copy(s, c).wait_recv()
            came, held = into[s, chunk(c), :].astype(F32), state[chunk(c), :]
            new = came + scale * held if s == 2 else scale * came + held
            out[s, chunk(c), :] = new.astype(BF16)
            c_copy(s, c).start()

    def accept(s):
        for c in range(CHUNKS):
            c_copy(s, c).wait_recv()

    def join():
        into[0] = (into[1].astype(F32) + told[1, 0:1, 0:1] * into[2].astype(F32)).astype(BF16)

    @pl.when(z < 4)
    def _():
        pl.semaphore_wait(barrier, 8)

    @pl.when(z == 0)
    def _():
        source(0)
        into[0] = jnp.zeros((DK, DV), BF16)

    @pl.when(z == 4)
    def _():
        source(1)

    @pl.when(z == 3)
    def _():
        source(2)

    @pl.when(z < 4)
    def _():
        for j, c in order:
            w_copy(j, c).start()

    loads[3].start()
    for c in own_w:
        c.start()
    loads[2].wait()
    t_at = lax.broadcasted_iota(jnp.int32, (SPAN, SPAN), 0)
    s_at = lax.broadcasted_iota(jnp.int32, (SPAN, SPAN), 1)
    for i in range(SPANS):
        mine = slice(i * SPAN, (i + 1) * SPAN)
        for j in range(i + 1):
            theirs = slice(j * SPAN, (j + 1) * SPAN)
            spread = col[mine, :] - cum_row[:, theirs]
            if i == j:
                spread = jnp.where(t_at >= s_at, spread, -1e30)
            scores = dot(q[mine, :], k[theirs, :], ((1,), (1,)))
            prob[:, theirs] = (scores * jnp.exp(spread)).astype(BF16)
        upto = (i + 1) * SPAN
        ret[mine, :] = dot(prob[:, :upto], v[:upto, :])

    loads[3].wait()

    def g_copy(i, j):
        here = gat.at[i, :, a_rows]
        return pltpu.make_async_remote_copy(
            src_ref=here, dst_ref=here, send_sem=g_s.at[i, j // 2], recv_sem=g_r.at[i, j // 2],
            device_id=a_peer(j), device_id_type=MESH,
        )

    def f_copy(i, j):
        cols = pl.ds(pl.multiple_of((a + 4 - j) % SIDE * DV, DV), DV)
        here = gat.at[i, pl.ds(j // 2 * (TILE // 2), TILE // 2), cols]
        return pltpu.make_async_remote_copy(
            src_ref=here, dst_ref=here, send_sem=f_s.at[i, j // 2], recv_sem=f_r.at[i, j // 2],
            device_id=a_peer(j), device_id_type=MESH,
        )

    def pass_on(i):
        for j in (1, 3):
            g_copy(i, j).wait_recv()
            f_copy(i, j).start()

    def gate(i):
        at = pl.ds(pl.multiple_of(i * TILE, TILE), TILE)
        r = ret[at, :] + jnp.exp(col[at, :]) * dot(q[at, :], into[0])
        r = r * lax.rsqrt(jnp.mean(r * r, axis=-1, keepdims=True) + 1e-6)
        u = g[at, :].astype(F32)
        gat[i, :, a_rows] = (u / (1.0 + jnp.exp(-u)) * r).astype(BF16)
        for j in (1, 3):
            g_copy(i, j).start()

    def start_gates():
        @pl.loop(0, AHEAD)
        def _(i):
            gate(i)

    @pl.when(z == 2)
    def _():
        relay(2)

    @pl.when((z == 5) | (z == 6))
    def _():
        relay(1)

    @pl.when(z == 0)
    def _():
        start_gates()

    @pl.when(z == 7)
    def _():
        share((0,))

    @pl.when((z >= 1) & (z <= 4))
    def _():
        relay(0)

    @pl.when(z <= 1)
    def _():
        relay(2)

    @pl.when(z == 0)
    def _():
        share((0,))

    @pl.when((z == 1) | (z == 2))
    def _():
        share((0, 1))

    @pl.when((z == 3) | (z == 4))
    def _():
        share((1,))

    @pl.when(z == 5)
    def _():
        accept(0)

    @pl.when(z == 6)
    def _():
        accept(2)
        join()

    @pl.when(z == 7)
    def _():
        @pl.loop(0, CHUNKS)
        def _(c):
            c_copy(2, c).wait_recv()
            c_copy(2, c, True).start()

        w_tell(1).wait_recv()
        accept(1)
        join()

    def p_copy(i, j):
        return pltpu.make_async_remote_copy(
            src_ref=part.at[i, j - 1], dst_ref=come.at[i, j - 1],
            send_sem=p_s.at[i, j - 1], recv_sem=p_r.at[i, j - 1],
            device_id=b_peer(j), device_id_type=MESH,
        )

    def project(i):
        for j in (1, 3):
            f_copy(i, j).wait_recv()
        heads = gat[i]
        for j in (2, 1, 3):
            part[i, j - 1] = dot(heads, wg[(b + j) % SIDE]).astype(BF16)
            p_copy(i, j).start()
        own[i] = dot(heads, wg[b])

    @pl.when(z > 0)
    def _():
        start_gates()

    @pl.loop(0, TILES + LAG)
    def _(i):
        @pl.when(i < TILES)
        def _():
            pass_on(i)

        @pl.when(i + AHEAD < TILES)
        def _():
            gate(i + AHEAD)

        @pl.when(i == LAG)
        def _():
            for c in own_w:
                c.wait()

            @pl.when(z < 4)
            def _():
                for j, c in order:
                    for u in (0, 1):
                        x_copy(u, j, c, True).wait_recv()

            @pl.when((z == 5) | (z == 6))
            def _():
                share(())

            @pl.when(z >= 4)
            def _():
                for j, c in order:
                    w_copy(j, c, True).wait_recv()

        @pl.when(i >= LAG)
        def _():
            project(i - LAG)

    @pl.loop(0, TILES)
    def _(i):
        for j in (1, 2, 3):
            p_copy(i, j).wait_recv()
        total = own[i]
        for j in (1, 2, 3):
            total = total + come[i, j - 1].astype(F32)
        o_ref[pl.ds(pl.multiple_of(i * TILE, TILE), TILE), :] = total.astype(BF16)

    def shared(u):
        for j, c in order:
            x_copy(u, j, c).wait_send()

    for j, c in order:
        w_copy(j, c).wait_send()

    @pl.when(z >= 4)
    def _():
        for j, c in order:
            w_copy(j, c, True).wait_send()

    @pl.when((z <= 2) | (z == 7))
    def _():
        shared(0)

    @pl.when((z >= 1) & (z <= 4))
    def _():
        shared(1)

    def sent(s):
        for c in range(CHUNKS):
            c_copy(s, c).wait_send()

    @pl.when(z <= 4)
    def _():
        sent(0)

    @pl.when((z >= 4) & (z <= 6))
    def _():
        sent(1)
        w_tell(1).wait_send()

    @pl.when((z <= 3) | (z == 7))
    def _():
        sent(2)

    @pl.when((z >= 1) & (z <= 3))
    def _():
        w_tell(2).wait_send()

    @pl.loop(0, TILES)
    def _(i):
        for j in (1, 3):
            g_copy(i, j).wait_send()
            f_copy(i, j).wait_send()
        for j in (1, 2, 3):
            p_copy(i, j).wait_send()


def layer(queries, keys, values, gates, decay_log, out_weight):
    dma = pltpu.SemaphoreType.DMA
    hbm = pl.BlockSpec(memory_space=pltpu.HBM)
    vmem = pl.BlockSpec(memory_space=pltpu.VMEM)
    return pl.pallas_call(
        kernel,
        out_shape=jax.ShapeDtypeStruct((BLOCK, COLS), BF16),
        in_specs=[hbm] * 4 + [vmem, hbm],
        out_specs=vmem,
        scratch_shapes=[
            pltpu.VMEM((BLOCK, DK), BF16),
            pltpu.VMEM((BLOCK, DK), BF16),
            pltpu.VMEM((BLOCK, DV), BF16),
            pltpu.VMEM((BLOCK, DV), BF16),
            pltpu.VMEM((SIDE, SIDE * DV, COLS), BF16),
            pltpu.VMEM((BLOCK, 1), F32),
            pltpu.VMEM((DK, DV), F32),
            pltpu.VMEM((3, DK, DV), BF16),
            pltpu.VMEM((3, DK, DV), BF16),
            pltpu.VMEM((3, 8, 128), F32),
            pltpu.VMEM((3, 8, 128), F32),
            pltpu.VMEM((SPAN, BLOCK), BF16),
            pltpu.VMEM((BLOCK, DV), F32),
            pltpu.VMEM((TILES, TILE, SIDE * DV), BF16),
            pltpu.VMEM((TILES, 3, TILE, COLS), BF16),
            pltpu.VMEM((TILES, 3, TILE, COLS), BF16),
            pltpu.VMEM((TILES, TILE, COLS), F32),
            dma((8,)),
            dma((2, 3, 2)), dma((2, 3, 2)),
            dma((2, 3, 2)), dma((2, 3, 2)),
            dma((3, CHUNKS)), dma((3, CHUNKS)),
            dma((3,)), dma((3,)),
            dma((TILES, 2)), dma((TILES, 2)),
            dma((TILES, 2)), dma((TILES, 2)),
            dma((TILES, 3)), dma((TILES, 3)),
        ],
        compiler_params=pltpu.CompilerParams(
            collective_id=0, has_side_effects=True, vmem_limit_bytes=53 * 2**20
        ),
        cost_estimate=pl.CostEstimate(
            flops=7 * 10**9, bytes_accessed=8 * 2**20, transcendentals=2 * 2**20
        ),
        name="retention",
    )(queries, keys, values, gates, decay_log, out_weight)


def solution(mesh):
    rows = P(("dp", "ctx"), "tp")
    placed = (rows, rows, rows, rows, P("tp", ("dp", "ctx")), P("tp", None))
    return jax.shard_map(layer, mesh=mesh, in_specs=placed, out_specs=rows, check_vma=False)
```
